32 devices in a mesh: tensor: 4 (over y, core), context: 8 (over z, x).
Axes of the slice: x: 2, y: 2, z: 4, core: 2. Of those that a mesh axis runs over, the one named last changes fastest.
Arguments:
- queries: bfloat16 [1024, 1024], P('tensor', 'context'), parts along dimension 0, may hold values from -6 to 6
- keys: bfloat16 [1024, 1024], P('tensor', 'context'), parts along dimension 0, may hold values from -6 to 6
- values: bfloat16 [1024, 1024], P('tensor', 'context'), parts along dimension 0, may hold values from -6 to 6
- filters: float32 [1024, 1024], P(('tensor', 'context')), parts along dimension 0, may hold values from -1 to 1
- skip: float32 [1024], P('tensor'), parts along dimension 0, may hold values from -3 to 3
Outputs:
- output: bfloat16 [1024, 1024], P('tensor', 'context'), parts along dimension 0
The draws below stay inside these ranges and needn't reach their ends.
There are 4 independent parts, one for each index of `tensor`. The reference program is written for one: setup_inputs(seed, part) draws one part's arguments, and reference() takes and returns one part's arrays. A program takes and returns all parts, laid end to end along the dimension named above; each array names one. Nothing has to cross between parts.
All inputs are finite; a program needn't handle non-finite values.
Results may differ from the reference program's by a relative error of at most 0.008.
Values may be sent and summed in bfloat16 or wider, within the bound.
No kernel may reach another device: no remote copies, remote signals or barrier semaphores. Data moves between devices by JAX's collectives and lax.ppermute only.
A program may use at most 64 MiB of HBM per device.

```python
import jax
import jax.numpy as jnp

C = 256
SEQ = 1024


def draw_filters(key, part):
    key_rate, key_noise = jax.random.split(jax.random.fold_in(key, 17), 2)
    lowest, highest = (0.5 / SEQ, 1.0 / 30.0)
    rates = jnp.exp(jax.random.uniform(key_rate, (C, 1), jnp.float32, jnp.log(lowest), jnp.log(highest)))
    amplitude = jnp.sqrt(1.0 - jnp.exp(-2.0 * rates))
    times = jnp.arange(SEQ, dtype=jnp.float32)[None, :]
    envelope = jnp.exp(-rates * times)
    noise = jnp.clip(jax.random.normal(key_noise, (C, SEQ), jnp.float32), -3.5, 3.5)
    return amplitude * noise * envelope


def level_of(stream_key, shape, shards, smallest, largest):
    loudness, own = 1.0, jax.random.fold_in(stream_key, 6)
    for position, shards_of in shards:
        heights = jnp.exp(jax.random.uniform(jax.random.fold_in(own, position), (shards_of,), jnp.float32, smallest / len(shards), largest / len(shards)))
        loudness = loudness * jnp.repeat(heights, shape[position] // shards_of).reshape([-1 if axis == position else 1 for axis in range(len(shape))])
    return loudness


def normal_values(own_key, extent, width, bound, cuts=(), kind=jnp.bfloat16):
    level = level_of(own_key, extent, cuts, -0.22, 0.18) if cuts else 1.0
    values = jax.random.normal(own_key, extent, jnp.float32) * width * level
    return jnp.minimum(jnp.maximum(values, -bound), bound).astype(kind)


def setup_inputs(seed: int = 0, part: int = 0) -> dict:
    key_list = jax.random.split(jax.random.key(seed), 6)
    part_splits = jax.random.split(jax.random.fold_in(key_list[5], part), 6)
    return {
        "queries": normal_values(part_splits[0], (C, SEQ), 1.0, 6.0, ((1, 8),)),
        "keys": normal_values(part_splits[1], (C, SEQ), 1.0, 6.0, ((1, 8),)),
        "values": normal_values(part_splits[2], (C, SEQ), 1.0, 6.0, ((1, 8),)),
        "filters": draw_filters(jax.random.fold_in(jax.random.fold_in(key_list[5], part), 71), part),
        "skip": normal_values(part_splits[4], (C,), 0.5, 3.0, (), jnp.float32),
    }


def reference(queries, keys, values, filters, skip):
    gated = (keys.astype(jnp.float32) * values.astype(jnp.float32)).astype(jnp.bfloat16)
    padded_len = 2 * SEQ
    spectrum = jnp.fft.rfft(gated.astype(jnp.float32), n=padded_len, axis=1) * jnp.fft.rfft(filters, n=padded_len, axis=1)
    convolved = jnp.fft.irfft(spectrum, n=padded_len, axis=1)[:, :SEQ].astype(jnp.bfloat16)
    output = queries.astype(jnp.float32) * (convolved.astype(jnp.float32) + skip[:, None] * gated.astype(jnp.float32))
    return output.astype(jnp.bfloat16)
```

```python
import functools
import math

import jax
import jax.numpy as jnp
import ml_dtypes
import numpy as np
from jax import lax
from jax.experimental import pallas as pl
from jax.experimental.pallas import tpu as pltpu
from jax.sharding import PartitionSpec as P

AXIS = "context"
HALVES = 2


def split_table(table):
    high = table.astype(ml_dtypes.bfloat16)
    low = (table - high.astype(np.float64)).astype(ml_dtypes.bfloat16)
    return high, low


def tables(block):
    full = 2 * block
    angles = np.pi * (2 * np.arange(block) + 1) / full
    signal = np.outer(np.arange(block), angles)
    taps = np.outer(np.arange(full) - block, angles)
    wx_high, wx_low = split_table(np.concatenate([np.cos(signal), -np.sin(signal)], axis=1))
    wf_high, wf_low = split_table(np.concatenate([np.cos(taps), -np.sin(taps)], axis=1))
    wy_high, wy_low = split_table(
        np.concatenate([np.cos(signal.T), -np.sin(signal.T)], axis=0) / block
    )
    return (
        np.concatenate([wx_high, wx_low], axis=0),
        np.concatenate([wf_high, wf_high, wf_low], axis=0),
        np.concatenate([wy_high, wy_high, wy_low], axis=0),
    )


def dot(left, right):
    return lax.dot_general(
        left, right, (((1,), (0,)), ((), ())), preferred_element_type=jnp.float32
    )


def split_dot(left, right):
    high = left.astype(jnp.bfloat16)
    low = (left - high.astype(jnp.float32)).astype(jnp.bfloat16)
    return dot(jnp.concatenate([high, low, high], axis=1), right)


def gate_kernel(keys_ref, values_ref, gated_ref, send_ref):
    peers, halves, rows, _ = send_ref.shape
    groups = peers // halves
    gated = (keys_ref[...].astype(jnp.float32) * values_ref[...].astype(jnp.float32)).astype(
        jnp.bfloat16
    )
    gated_ref[...] = gated
    for half in range(halves):
        for group in range(groups):
            start = (half * groups + group) * rows
            part = gated[start : start + rows]
            for copy in range(halves):
                send_ref[copy * groups + group, half] = part


def taps_kernel(own_ref, other_ref, table_ref, gated_ref, skip_ref, taps_ref, skipped_ref):
    half = lax.axis_index(AXIS) // (lax.axis_size(AXIS) // HALVES)
    shards, _, rows, full = taps_ref.shape
    block = full // 2
    table = table_ref[...]
    for which, ref in ((half, own_ref), (1 - half, other_ref)):
        padded = jnp.concatenate([jnp.zeros((rows, block), jnp.float32), ref[...]], axis=1)
        windows = jnp.concatenate(
            [padded[:, m * block : m * block + full] for m in range(shards)], axis=0
        )
        spectra = split_dot(windows, table)
        for m in range(shards):
            taps_ref[m, which] = spectra[m * rows : (m + 1) * rows]
    skipped_ref[...] = skip_ref[...] * gated_ref[...].astype(jnp.float32)


def conv_kernel(arrived_ref, taps_ref, wx_ref, wy_ref, *refs):
    outs, signal_ref, product_ref = refs[:-2], refs[-2], refs[-1]
    shards, halves, rows, block = arrived_ref.shape
    groups = shards // halves
    index = lax.axis_index(AXIS)
    half, group = index // groups, lax.rem(index, groups)
    chans = halves * rows
    arrived = arrived_ref[...].reshape(shards * chans, block)
    signal_ref[...] = dot(jnp.concatenate([arrived, arrived], axis=1), wx_ref[...])

    for part in range(halves):

        @pl.when(half == part)
        def _():
            for piece in range(chans // 8):
                which, at = piece * 8 // rows, piece * 8 % rows
                taps_re = []
                taps_im = []
                last = (part + 1) * groups
                for m in range(last):
                    tap = taps_ref[m, which, at : at + 8, :]
                    taps_re.append(tap[:, :block])
                    taps_im.append(tap[:, block:])
                total_re = [None] * groups
                total_im = [None] * groups
                for b in range(last):
                    row = b * chans + piece * 8
                    wave = signal_ref[row : row + 8, :]
                    re, im = wave[:, :block], wave[:, block:]
                    for g in range(groups):
                        m = part * groups + g - b
                        if m < 0:
                            continue
                        new_re = re * taps_re[m] - im * taps_im[m]
                        new_im = re * taps_im[m] + im * taps_re[m]
                        total_re[g] = new_re if b == 0 else total_re[g] + new_re
                        total_im[g] = new_im if b == 0 else total_im[g] + new_im
                for g in range(groups):
                    row = g * chans + piece * 8
                    product_ref[row : row + 8, :block] = total_re[g]
                    product_ref[row : row + 8, block:] = total_im[g]

    for k, out_ref in enumerate(outs):
        start = pl.multiple_of((group ^ k) * chans, chans)
        spectrum = product_ref[pl.ds(start, chans), :]
        out_ref[...] = split_dot(spectrum, wy_ref[...]).astype(jnp.bfloat16)


def final_kernel(queries_ref, skipped_ref, *refs):
    parts, out_ref = refs[:-1], refs[-1]
    groups = len(parts)
    group = lax.rem(lax.axis_index(AXIS), groups)
    rows = parts[0].shape[0] // HALVES
    for k, part_ref in enumerate(parts):
        for half in range(HALVES):
            start = pl.multiple_of((half * groups + (group ^ k)) * rows, rows)
            place = pl.ds(start, rows)
            total = (
                part_ref[half * rows : (half + 1) * rows, :].astype(jnp.float32)
                + skipped_ref[place, :]
            )
            out_ref[place, :] = (queries_ref[place, :].astype(jnp.float32) * total).astype(
                jnp.bfloat16
            )


def call(kernel, outs, args, scratch=()):
    vmem = pl.BlockSpec(memory_space=pltpu.VMEM)
    return pl.pallas_call(
        kernel,
        out_shape=[jax.ShapeDtypeStruct(shape, dtype) for shape, dtype in outs],
        in_specs=[vmem] * len(args),
        out_specs=[vmem] * len(outs),
        scratch_shapes=list(scratch),
        compiler_params=pltpu.CompilerParams(vmem_limit_bytes=48 * 1024 * 1024),
    )(*args)


def per_device(queries, keys, values, filters, skip):
    channels, block = keys.shape
    shards = lax.axis_size(AXIS)
    groups = shards // HALVES
    rows = channels // shards
    chans = HALVES * rows
    wx, wf, wy = (jnp.asarray(table) for table in tables(block))
    f32, bf16 = jnp.float32, jnp.bfloat16

    other = lax.ppermute(filters, AXIS, [(i, i ^ groups) for i in range(shards)])
    gated, send = call(
        gate_kernel,
        [((channels, block), bf16), ((shards, HALVES, rows, block), bf16)],
        (keys, values),
    )
    arrived = lax.all_to_all(send, AXIS, split_axis=0, concat_axis=0, tiled=True)
    spread = jnp.broadcast_to(skip[:, None], (channels, block))
    taps, skipped = call(
        taps_kernel,
        [((shards, HALVES, rows, 2 * block), f32), ((channels, block), f32)],
        (filters, other, wf, gated, spread),
    )
    parts = call(
        conv_kernel,
        [((chans, block), bf16)] * groups,
        (arrived, taps, wx, wy),
        [
            pltpu.VMEM((shards * chans, 2 * block), f32),
            pltpu.VMEM((groups * chans, 2 * block), f32),
        ],
    )
    returned = list(parts)
    for k in range(groups - 1, 0, -1):
        returned[k] = lax.ppermute(parts[k], AXIS, [(i, i ^ k) for i in range(shards)])
    return call(final_kernel, [((channels, block), bf16)], (queries, skipped, *returned))[0]


def solution(mesh):
    placed = (
        P("tensor", AXIS),
        P("tensor", AXIS),
        P("tensor", AXIS),
        P(("tensor", AXIS), None),
        P("tensor"),
    )
    return jax.shard_map(
        per_device, mesh=mesh, in_specs=placed, out_specs=P("tensor", AXIS), check_vma=False
    )
```

```python
import jax
import jax.numpy as jnp
import ml_dtypes
import numpy as np
from jax import lax
from jax.experimental import pallas as pl
from jax.experimental.pallas import tpu as pltpu
from jax.sharding import PartitionSpec as P

AXIS = "context"
HALVES = 2


def split_table(table):
    high = table.astype(ml_dtypes.bfloat16)
    low = (table - high.astype(np.float64)).astype(ml_dtypes.bfloat16)
    return high, low


def transform_table(block):
    full = 2 * block
    angles = np.pi * (2 * np.arange(block) + 1) / full
    signal = np.outer(np.arange(block), angles)
    taps = np.outer(np.arange(full) - block, angles)
    forward = split_table(np.concatenate([np.cos(signal), -np.sin(signal)], axis=1))
    window = split_table(np.concatenate([np.cos(taps), -np.sin(taps)], axis=1))
    back = split_table(np.concatenate([np.cos(signal.T), -np.sin(signal.T)], axis=0) / block)
    return np.concatenate([*forward, *window, np.concatenate(back, axis=1)], axis=0)


def dot(left, right):
    return lax.dot_general(
        left, right, (((1,), (0,)), ((), ())), preferred_element_type=jnp.float32
    )


def split_dot(left, high_table, low_table):
    high = left.astype(jnp.bfloat16)
    low = (left - high.astype(jnp.float32)).astype(jnp.bfloat16)
    return dot(high, high_table) + dot(low, high_table) + dot(high, low_table)


def place():
    index = lax.axis_index(AXIS)
    groups = lax.axis_size(AXIS) // HALVES
    return index // groups, lax.rem(index, groups)


def prepare_kernel(gated_ref, filters_ref, coarse_ref, *sends):
    coarse_ref[...] = filters_ref[...].astype(jnp.bfloat16)
    groups = len(sends)
    _, group = place()
    rows = sends[0].shape[0] // HALVES
    for k, send_ref in enumerate(sends):
        for half in range(HALVES):
            start = pl.multiple_of((half * groups + (group ^ k)) * rows, rows)
            send_ref[half * rows : (half + 1) * rows, :] = gated_ref[pl.ds(start, rows), :]


def taps_of(own_ref, other_ref, table_ref, taps_ref):
    half, _ = place()
    shards, _, rows, full = taps_ref.shape
    block = full // 2
    for which, ref in ((half, own_ref), (1 - half, other_ref)):
        padded = jnp.concatenate(
            [jnp.zeros((rows, block), jnp.float32), ref[...].astype(jnp.float32)], axis=1
        )
        windows = jnp.concatenate(
            [padded[:, m * block : m * block + full] for m in range(shards)], axis=0
        )
        spectra = split_dot(windows, table_ref[full : 2 * full, :], table_ref[2 * full : 3 * full, :])
        for m in range(shards):
            taps_ref[m, which] = spectra[m * rows : (m + 1) * rows]


def signal_of(blocks_ref, table_ref):
    block = blocks_ref.shape[-1]
    stacked = blocks_ref[...].reshape(-1, block)
    return dot(jnp.concatenate([stacked, stacked], axis=1), table_ref[: 2 * block, :])


def products(signal_ref, taps_ref, shift, shape, store):
    groups, chans, block = shape
    rows = chans // HALVES
    for piece in range(chans // 8):
        which, at = piece * 8 // rows, piece * 8 % rows
        waves = [signal_ref[b * chans + piece * 8 : b * chans + piece * 8 + 8, :] for b in range(groups)]
        for j in range(groups):
            total_re = total_im = None
            for b in range(groups):
                if shift + j < b:
                    continue
                tap = taps_ref[shift + j - b, which, at : at + 8, :]
                re, im = waves[b][:, :block], waves[b][:, block:]
                tap_re, tap_im = tap[:, :block], tap[:, block:]
                new_re = re * tap_re - im * tap_im
                new_im = re * tap_im + im * tap_re
                total_re = new_re if total_re is None else total_re + new_re
                total_im = new_im if total_im is None else total_im + new_im
            store(slice(j * chans + piece * 8, j * chans + piece * 8 + 8), total_re, total_im)


def stack_kernel(*refs):
    arrived, blocks_ref = refs[:-1][::-1], refs[-1]
    _, group = place()
    for k, ref in enumerate(arrived):
        blocks_ref[group ^ k] = ref[...]


def near_kernel(own_ref, other_ref, blocks_ref, table_ref, gated_ref, skip_ref, taps_ref, product_ref, skipped_ref, signal_ref):
    skipped_ref[...] = skip_ref[...] * gated_ref[...].astype(jnp.float32)
    block = blocks_ref.shape[-1]
    taps_of(own_ref, other_ref, table_ref, taps_ref)
    signal_ref[...] = signal_of(blocks_ref, table_ref)

    def store(at, re, im):
        product_ref[at, :block] = re
        product_ref[at, block:] = im

    products(signal_ref, taps_ref, 0, blocks_ref.shape, store)


def far_kernel(taps_ref, blocks_ref, near_ref, table_ref, *refs):
    outs, signal_ref, product_ref = refs[:-2], refs[-2], refs[-1]
    half, group = place()
    groups, chans, block = blocks_ref.shape
    full = 2 * block

    @pl.when(half == 0)
    def _():
        product_ref[...] = near_ref[...]

    @pl.when(half > 0)
    def _():
        signal_ref[...] = signal_of(blocks_ref, table_ref)

        def store(at, re, im):
            product_ref[at, :block] = near_ref[at, :block] + re
            product_ref[at, block:] = near_ref[at, block:] + im

        products(signal_ref, taps_ref, groups, blocks_ref.shape, store)

    back = table_ref[3 * full : 4 * full, :]
    for k, out_ref in enumerate(outs):
        start = pl.multiple_of((group ^ k) * chans, chans)
        spectrum = product_ref[pl.ds(start, chans), :]
        out_ref[...] = split_dot(spectrum, back[:, :block], back[:, block:]).astype(jnp.bfloat16)


def final_kernel(queries_ref, skipped_ref, *refs):
    parts, out_ref = refs[:-1][::-1], refs[-1]
    groups = len(parts)
    _, group = place()
    rows = parts[0].shape[0] // HALVES
    for k, part_ref in enumerate(parts):
        for half in range(HALVES):
            start = pl.multiple_of((half * groups + (group ^ k)) * rows, rows)
            where = pl.ds(start, rows)
            total = (
                part_ref[half * rows : (half + 1) * rows, :].astype(jnp.float32)
                + skipped_ref[where, :]
            )
            out_ref[where, :] = (queries_ref[where, :].astype(jnp.float32) * total).astype(
                jnp.bfloat16
            )


def call(kernel, outs, args, scratch=()):
    vmem = pl.BlockSpec(memory_space=pltpu.VMEM)
    return pl.pallas_call(
        kernel,
        out_shape=[jax.ShapeDtypeStruct(shape, dtype) for shape, dtype in outs],
        in_specs=[vmem] * len(args),
        out_specs=[vmem] * len(outs),
        scratch_shapes=list(scratch),
        compiler_params=pltpu.CompilerParams(vmem_limit_bytes=16 * 1024 * 1024),
    )(*args)


def per_device(queries, keys, values, filters, skip):
    channels, block = keys.shape
    shards = lax.axis_size(AXIS)
    groups = shards // HALVES
    rows = channels // shards
    chans = HALVES * rows
    f32, bf16 = jnp.float32, jnp.bfloat16
    table = jnp.asarray(transform_table(block))
    swap = lambda x, k: lax.ppermute(x, AXIS, [(i, i ^ k) for i in range(shards)])

    gated = (keys.astype(f32) * values.astype(f32)).astype(bf16)
    coarse, *sends = call(
        prepare_kernel,
        [(filters.shape, bf16)] + [((chans, block), bf16)] * groups,
        (gated, filters),
    )
    other = swap(coarse, groups)
    arrived = [swap(sends[k], k) if k else sends[k] for k in range(groups - 1, -1, -1)]
    (own,) = call(stack_kernel, [((groups, chans, block), bf16)], arrived)
    across = swap(own, groups)
    spread = jnp.broadcast_to(skip[:, None], (channels, block))
    taps, product, skipped = call(
        near_kernel,
        [((shards, HALVES, rows, 2 * block), f32), ((groups * chans, 2 * block), f32), ((channels, block), f32)],
        (filters, other, own, table, gated, spread),
        [pltpu.VMEM((groups * chans, 2 * block), f32)],
    )
    parts = call(
        far_kernel,
        [((chans, block), bf16)] * groups,
        (taps, across, product, table),
        [pltpu.VMEM((groups * chans, 2 * block), f32)] * 2,
    )
    returned = [swap(parts[k], k) if k else parts[k] for k in range(groups - 1, -1, -1)]
    return call(final_kernel, [((channels, block), bf16)], (queries, skipped, *returned))[0]


def solution(mesh):
    placed = (
        P("tensor", AXIS),
        P("tensor", AXIS),
        P("tensor", AXIS),
        P(("tensor", AXIS), None),
        P("tensor"),
    )
    return jax.shard_map(
        per_device, mesh=mesh, in_specs=placed, out_specs=P("tensor", AXIS), check_vma=False
    )
```

```python
import jax
import jax.numpy as jnp
import ml_dtypes
import numpy as np
from jax import lax
from jax.experimental import pallas as pl
from jax.experimental.pallas import tpu as pltpu
from jax.sharding import PartitionSpec as P

AXIS = "context"
HALVES = 2


def transform_table(block):
    angles = np.pi * np.outer(np.arange(block), 2 * np.arange(block) + 1) / (2 * block)
    table = np.concatenate([np.cos(angles), -np.sin(angles)], axis=1)
    high = table.astype(ml_dtypes.bfloat16)
    low = (table - high.astype(np.float64)).astype(ml_dtypes.bfloat16)
    return np.concatenate([high, low], axis=0)


def dot(left, right, turned=False):
    dims = (((1,), (1 if turned else 0,)), ((), ()))
    return lax.dot_general(left, right, dims, preferred_element_type=jnp.float32)


def split(values):
    high = values.astype(jnp.bfloat16)
    return high, (values - high.astype(jnp.float32)).astype(jnp.bfloat16)


def place():
    index = lax.axis_index(AXIS)
    groups = lax.axis_size(AXIS) // HALVES
    return index // groups, lax.rem(index, groups)


def span(start, size):
    return pl.ds(pl.multiple_of(start * size, size), size)


def store_waves(blocks, table_ref, waves_refs):
    _, group = place()
    rows = waves_refs[0].shape[1]
    stacked = jnp.concatenate(blocks, axis=0)
    spectra = dot(jnp.concatenate([stacked, stacked], axis=1), table_ref[...])
    parts = len(waves_refs)
    for k in range(len(blocks) // parts):
        for i, ref in enumerate(waves_refs):
            at = (k * parts + i) * rows
            ref[group ^ k] = spectra[at : at + rows]


def store_taps(taps, table_ref, taps_ref):
    count, rows, full = taps_ref.shape
    block = full // 2
    high, low = split(jnp.concatenate(taps, axis=0))
    spectra = dot(jnp.concatenate([high, high], axis=1), table_ref[...]) + dot(
        low, table_ref[:block, :]
    )
    odd = lax.rem(lax.broadcasted_iota(jnp.int32, (rows, block), 1), 2)
    sign = 1.0 - 2.0 * odd.astype(jnp.float32)
    for m in range(count):
        now = spectra[m * rows : (m + 1) * rows]
        if m == 0:
            taps_ref[m] = now
            continue
        past = spectra[(m - 1) * rows : m * rows]
        taps_ref[m, :, :block] = now[:, :block] - sign * past[:, block:]
        taps_ref[m, :, block:] = now[:, block:] + sign * past[:, :block]


def back_from(spectra, table_ref):
    block = spectra.shape[1] // 2
    high, low = split(spectra)
    top, rest = table_ref[:block, :], table_ref[block:, :]
    total = dot(high, top, True) + dot(low, top, True) + dot(high, rest, True)
    return total * (1.0 / block)


def products(waves_ref, taps_ref, shift, out_ref, start=None):
    groups, rows, full = waves_ref.shape
    block = full // 2
    for at in range(0, rows, 8):
        part = slice(at, at + 8)
        waves = [waves_ref[b, part, :] for b in range(groups)]
        for j in range(groups):
            total = [None, None]
            if start is not None:
                total = [start[j, part, :block], start[j, part, block:]]
            for b in range(groups):
                if shift + j < b:
                    continue
                tap = taps_ref[shift + j - b, part, :]
                re, im = waves[b][:, :block], waves[b][:, block:]
                tap_re, tap_im = tap[:, :block], tap[:, block:]
                new = [re * tap_re - im * tap_im, re * tap_im + im * tap_re]
                total = [n if t is None else t + n for t, n in zip(total, new)]
            out_ref[j, part, :block] = total[0]
            out_ref[j, part, block:] = total[1]


def prepare_kernel(*refs):
    sources, targets, (gated_ref, coarse_ref) = refs[:6], refs[6:10], refs[10:12]
    sends, (keys_ref, values_ref, sem) = refs[12:-3], refs[-3:]
    near_ref, block = targets[0], gated_ref.shape[1]
    copies = [
        pltpu.make_async_copy(source, target, sem.at[i])
        for i, (source, target) in enumerate(zip(sources, (keys_ref, values_ref, *targets)))
    ]
    for copy in copies:
        copy.start()
    copies[0].wait()
    copies[1].wait()
    gated_ref[...] = (
        keys_ref[...].astype(jnp.float32) * values_ref[...].astype(jnp.float32)
    ).astype(jnp.bfloat16)
    groups = len(sends)
    _, group = place()
    rows = sends[0].shape[0] // HALVES
    for k, send_ref in enumerate(sends):
        for half in range(HALVES):
            send_ref[half * rows : (half + 1) * rows, :] = gated_ref[
                span(half * groups + (group ^ k), rows), :
            ]
    copies[2].wait()
    for m in range(near_ref.shape[1] // block):
        coarse_ref[m * rows : (m + 1) * rows, :] = near_ref[
            :, m * block : (m + 1) * block
        ].astype(jnp.bfloat16)
    for copy in copies[3:]:
        copy.wait()


def stack_kernel(*refs):
    arrived, out_ref = refs[:-1][::-1], refs[-1]
    chans = arrived[0].shape[0]
    for k, ref in enumerate(arrived):
        out_ref[k * chans : (k + 1) * chans, :] = ref[...]


def halves_of(blocks):
    half, _ = place()
    rows = blocks[0].shape[0] // HALVES
    parts = []
    for ref in blocks:
        parts += [ref[span(half, rows), :], ref[span(1 - half, rows), :]]
    return parts


def own_kernel(table_ref, own_ref, gated_ref, skip_ref, *refs):
    arrived, (taps_ref, waves_ref, sums_ref, skipped_ref, own_waves_ref) = refs[:-5][::-1], refs[-5:]
    block = gated_ref.shape[1]
    store_taps(
        [own_ref[:, m * block : (m + 1) * block] for m in range(taps_ref.shape[0])],
        table_ref,
        taps_ref,
    )
    store_waves(halves_of(arrived), table_ref, [own_waves_ref, waves_ref])
    products(own_waves_ref, taps_ref, 0, sums_ref)
    spread = jnp.broadcast_to(skip_ref[...][None, :], (block, gated_ref.shape[0])).T
    skipped_ref[...] = spread * gated_ref[...].astype(jnp.float32)


def other_kernel(table_ref, other_ref, waves_ref, taps_ref, sums_ref):
    rows = waves_ref.shape[1]
    store_taps(
        [
            other_ref[m * rows : (m + 1) * rows, :].astype(jnp.float32)
            for m in range(taps_ref.shape[0])
        ],
        table_ref,
        taps_ref,
    )
    products(waves_ref, taps_ref, 0, sums_ref)


def store_back(own_ref, other_ref, table_ref, back_ref, outs):
    half, group = place()
    groups, rows, full = own_ref.shape
    spectra = [ref[...].reshape(groups * rows, full) for ref in (own_ref, other_ref)]
    back = back_from(jnp.concatenate(spectra, axis=0), table_ref)
    back_ref[...] = back.astype(jnp.bfloat16).reshape(back_ref.shape)
    for k, out_ref in enumerate(outs):
        out_ref[span(half, rows), :] = back_ref[group ^ k]
        out_ref[span(1 - half, rows), :] = back_ref[groups + (group ^ k)]


def near_kernel(table_ref, own_ref, other_ref, *refs):
    store_back(own_ref, other_ref, table_ref, refs[-1], refs[:-1])


def far_kernel(table_ref, own_taps_ref, taps_ref, own_ref, other_ref, across_ref, *refs):
    outs, (own_waves_ref, waves_ref, own_sums_ref, sums_ref, back_ref) = refs[:-5], refs[-5:]
    groups, rows, _ = own_ref.shape
    chans = HALVES * rows
    blocks = [across_ref.at[k * chans : (k + 1) * chans, :] for k in range(groups)]
    store_waves(halves_of(blocks), table_ref, [own_waves_ref, waves_ref])
    products(own_waves_ref, own_taps_ref, groups, own_sums_ref, own_ref)
    products(waves_ref, taps_ref, groups, sums_ref, other_ref)
    store_back(own_sums_ref, sums_ref, table_ref, back_ref, outs)


def join_kernel(*refs):
    parts, out_ref = refs[:-1][::-1], refs[-1]
    groups = len(parts)
    _, group = place()
    rows = parts[0].shape[0] // HALVES
    for k, part_ref in enumerate(parts):
        for half in range(HALVES):
            out_ref[span(half * groups + (group ^ k), rows), :] = part_ref[
                half * rows : (half + 1) * rows, :
            ]


def copy_kernel(in_ref, out_ref):
    out_ref[...] = in_ref[...]


def final_kernel(queries_ref, skipped_ref, convolved_ref, out_ref):
    total = convolved_ref[...].astype(jnp.float32) + skipped_ref[...]
    out_ref[...] = (queries_ref[...].astype(jnp.float32) * total).astype(jnp.bfloat16)


VMEM = pl.BlockSpec(memory_space=pltpu.VMEM)
HBM = pl.BlockSpec(memory_space=pltpu.HBM)


def call(kernel, outs, args, scratch=(), far=0):
    args = [
        pltpu.with_memory_space_constraint(arg, pltpu.HBM) if i < far else arg
        for i, arg in enumerate(args)
    ]
    return pl.pallas_call(
        kernel,
        out_shape=[jax.ShapeDtypeStruct(shape, dtype) for shape, dtype in outs],
        in_specs=[HBM if i < far else VMEM for i in range(len(args))],
        out_specs=[VMEM] * len(outs),
        scratch_shapes=list(scratch),
        compiler_params=pltpu.CompilerParams(vmem_limit_bytes=16 * 1024 * 1024),
    )(*args)


def per_device(queries, keys, values, filters, skip):
    channels, block = keys.shape
    shards = lax.axis_size(AXIS)
    groups = shards // HALVES
    rows = channels // shards
    chans = HALVES * rows
    full = 2 * block
    f32, bf16 = jnp.float32, jnp.bfloat16
    table = jnp.asarray(transform_table(block))
    swap = lambda x, k: lax.ppermute(x, AXIS, [(i, i ^ k) for i in range(shards)])
    whole = ((channels, block), bf16)
    group_part = ((chans, block), bf16)
    spectra = ((groups, rows, full), f32)
    outputs = ((shards, rows, block), bf16)
    all_taps = ((shards, rows, full), f32)
    scratch = lambda *shapes: [pltpu.VMEM(*shape) for shape in shapes]

    near = (filters, skip, table, queries)
    own, skip, table, queries, gated, coarse, *sends = call(
        prepare_kernel,
        [(x.shape, x.dtype) for x in near] + [whole, whole] + [group_part] * groups,
        (keys, values, *near),
        scratch(whole, whole) + [pltpu.SemaphoreType.DMA((6,))],
        6,
    )
    other = swap(coarse, groups)
    arrived = [swap(sends[k], k) if k else sends[k] for k in range(groups - 1, -1, -1)]
    (stacked,) = call(stack_kernel, [whole], arrived)
    across = swap(stacked, groups)
    taps, waves, own_sums, skipped = call(
        own_kernel,
        [all_taps, spectra, spectra, ((channels, block), f32)],
        (table, own, gated, skip, *arrived),
        scratch(spectra),
    )
    other_taps, other_sums = call(other_kernel, [all_taps, spectra], (table, other, waves))

    def give_back(parts):
        returned = [swap(parts[k], k) if k else parts[k] for k in range(groups - 1, -1, -1)]
        return call(join_kernel, [whole], returned)[0]

    def early():
        return give_back(
            call(
                near_kernel, [group_part] * groups, (table, own_sums, other_sums), scratch(outputs)
            ),
        )

    def late(across):
        return give_back(
            call(
                far_kernel,
                [group_part] * groups,
                (table, taps, other_taps, own_sums, other_sums, across),
                scratch(spectra, spectra, spectra, spectra, outputs)
            )
        )

    copy = lambda x: call(copy_kernel, [whole], (x,))[0]
    first = lax.axis_index(AXIS) < groups
    convolved = lax.cond(first, early, lambda: copy(gated))
    convolved = lax.cond(
        first, lambda done, _: copy(done), lambda _, across: late(across), convolved, across
    )
    return call(final_kernel, [whole], (queries, skipped, convolved))[0]


def solution(mesh):
    placed = (
        P("tensor", AXIS),
        P("tensor", AXIS),
        P("tensor", AXIS),
        P(("tensor", AXIS), None),
        P("tensor"),
    )
    return jax.shard_map(
        per_device, mesh=mesh, in_specs=placed, out_specs=P("tensor", AXIS), check_vma=False
    )
```

```python
import jax
import jax.numpy as jnp
import ml_dtypes
import numpy as np
from jax import lax
from jax.experimental import pallas as pl
from jax.experimental.pallas import tpu as pltpu
from jax.sharding import PartitionSpec as P

AXIS = "context"
HALVES = 2


def transform_table(block):
    angles = np.pi * np.outer(np.arange(block), 2 * np.arange(block) + 1) / (2 * block)
    table = np.concatenate([np.cos(angles), -np.sin(angles)], axis=1)
    high = table.astype(ml_dtypes.bfloat16)
    low = (table - high.astype(np.float64)).astype(ml_dtypes.bfloat16)
    return np.concatenate([high, low], axis=0)


def dot(left, right, turned=False):
    dims = (((1,), (1 if turned else 0,)), ((), ()))
    return lax.dot_general(left, right, dims, preferred_element_type=jnp.float32)


def split(values):
    high = values.astype(jnp.bfloat16)
    return high, (values - high.astype(jnp.float32)).astype(jnp.bfloat16)


def place():
    index = lax.axis_index(AXIS)
    groups = lax.axis_size(AXIS) // HALVES
    return index // groups, lax.rem(index, groups)


def span(start, size):
    return pl.ds(pl.multiple_of(start * size, size), size)


def store_waves(blocks, table_ref, waves_refs):
    _, group = place()
    rows = waves_refs[0].shape[1]
    stacked = jnp.concatenate(blocks, axis=0)
    spectra = dot(jnp.concatenate([stacked, stacked], axis=1), table_ref[...])
    parts = len(waves_refs)
    for k in range(len(blocks) // parts):
        for i, ref in enumerate(waves_refs):
            at = (k * parts + i) * rows
            ref[group ^ k] = spectra[at : at + rows]


def store_taps(taps, table_ref, taps_ref):
    count, rows, full = taps_ref.shape
    block = full // 2
    high, low = split(jnp.concatenate(taps, axis=0))
    spectra = dot(jnp.concatenate([high, high], axis=1), table_ref[...]) + dot(
        low, table_ref[:block, :]
    )
    odd = lax.rem(lax.broadcasted_iota(jnp.int32, (rows, block), 1), 2)
    sign = 1.0 - 2.0 * odd.astype(jnp.float32)
    for m in range(count):
        now = spectra[m * rows : (m + 1) * rows]
        if m == 0:
            taps_ref[m] = now
            continue
        past = spectra[(m - 1) * rows : m * rows]
        taps_ref[m, :, :block] = now[:, :block] - sign * past[:, block:]
        taps_ref[m, :, block:] = now[:, block:] + sign * past[:, :block]


def back_from(spectra, table_ref):
    block = spectra.shape[1] // 2
    high, low = split(spectra)
    top, rest = table_ref[:block, :], table_ref[block:, :]
    total = dot(high, top, True) + dot(low, top, True) + dot(high, rest, True)
    return total * (1.0 / block)


def products(waves_ref, taps_ref, shift, out_ref, start=None):
    groups, rows, full = waves_ref.shape
    block = full // 2
    for at in range(0, rows, 8):
        part = slice(at, at + 8)
        waves = [waves_ref[b, part, :] for b in range(groups)]
        for j in range(groups):
            total = [None, None]
            if start is not None:
                total = [start[j, part, :block], start[j, part, block:]]
            for b in range(groups):
                if shift + j < b:
                    continue
                tap = taps_ref[shift + j - b, part, :]
                re, im = waves[b][:, :block], waves[b][:, block:]
                tap_re, tap_im = tap[:, :block], tap[:, block:]
                new = [re * tap_re - im * tap_im, re * tap_im + im * tap_re]
                total = [n if t is None else t + n for t, n in zip(total, new)]
            out_ref[j, part, :block] = total[0]
            out_ref[j, part, block:] = total[1]


def prepare_kernel(*refs):
    sources, targets, (gated_ref, coarse_ref) = refs[:6], refs[6:10], refs[10:12]
    sends, (keys_ref, values_ref, sem) = refs[12:-3], refs[-3:]
    near_ref, block = targets[0], gated_ref.shape[1]
    half, group = place()
    copies = [
        pltpu.make_async_copy(source, target, sem.at[i])
        for i, (source, target) in enumerate(zip(sources, (keys_ref, values_ref, *targets)))
    ]
    for copy in copies:
        copy.start()
    copies[0].wait()
    copies[1].wait()
    gated_ref[...] = (
        keys_ref[...].astype(jnp.float32) * values_ref[...].astype(jnp.float32)
    ).astype(jnp.bfloat16)
    groups = len(sends)
    rows = sends[0].shape[0] // HALVES
    for k, send_ref in enumerate(sends):
        for part in range(HALVES):
            send_ref[part * rows : (part + 1) * rows, :] = gated_ref[
                span(part * groups + (group ^ k), rows), :
            ]
    copies[2].wait()
    coarse_ref[:rows, :] = sends[0][span(1 - half, rows), :]
    for m in range(groups):
        parts = split(near_ref[:, m * block : (m + 1) * block])
        coarse_ref[(m + 1) * rows : (m + 2) * rows, :] = parts[0]
        at = (groups + 1 + m) * rows
        if at < coarse_ref.shape[0]:
            coarse_ref[at : at + rows, :] = parts[1]
    for copy in copies[3:]:
        copy.wait()


def lead_kernel(table_ref, own_ref, *refs):
    arrived, (out_ref, taps_ref, waves_ref, sums_ref) = refs[:-4][::-1], refs[-4:]
    half, _ = place()
    groups, rows, full = waves_ref.shape
    block = full // 2

    @pl.when(half == 0)
    def _():
        for k, ref in enumerate(arrived[1:]):
            out_ref[(groups + k) * rows : (groups + k + 1) * rows, :] = ref[rows:, :]
        store_taps(
            [own_ref[:, m * block : (m + 1) * block] for m in range(taps_ref.shape[0])],
            table_ref,
            taps_ref,
        )
        store_waves([ref[:rows, :] for ref in arrived], table_ref, [waves_ref])
        products(waves_ref, taps_ref, groups, sums_ref)
        sums = sums_ref[...].reshape(groups * rows, full)
        out_ref[: groups * rows, :] = back_from(sums, table_ref).astype(jnp.bfloat16)


def store_parts(own, other, outs):
    half, group = place()
    rows = outs[0].shape[0] // HALVES
    for k, out_ref in enumerate(outs):
        out_ref[span(half, rows), :] = own(group ^ k).astype(jnp.bfloat16)
        out_ref[span(1 - half, rows), :] = other(group ^ k).astype(jnp.bfloat16)


def near_kernel(table_ref, own_ref, other_ref, gated_ref, skip_ref, *refs):
    groups = (len(refs) - 8) // 2
    arrived, parts = refs[:groups][::-1], refs[groups : 2 * groups]
    taps_ref, sums_ref, out_ref, skipped_ref = refs[2 * groups : 2 * groups + 4]
    other_taps_ref, own_waves_ref, waves_ref, other_sums_ref = refs[2 * groups + 4 :]
    half, _ = place()
    _, rows, full = sums_ref.shape
    block = full // 2
    store_taps(
        [own_ref[:, m * block : (m + 1) * block] for m in range(taps_ref.shape[0])],
        table_ref,
        taps_ref,
    )
    other_taps = []
    for m in range(groups):
        tap = other_ref[(m + 1) * rows : (m + 2) * rows, :].astype(jnp.float32)
        at = (groups + 1 + m) * rows
        if at < other_ref.shape[0]:
            tap = tap + other_ref[at : at + rows, :].astype(jnp.float32)
        other_taps.append(tap)
    store_taps(other_taps, table_ref, other_taps_ref)
    blocks = []
    for ref in arrived:
        blocks += [ref[span(half, rows), :], ref[span(1 - half, rows), :]]
    store_waves(blocks, table_ref, [own_waves_ref, waves_ref])
    products(own_waves_ref, taps_ref, 0, sums_ref)
    products(waves_ref, other_taps_ref, 0, other_sums_ref)
    spectra = [ref[...].reshape(groups * rows, full) for ref in (other_sums_ref, sums_ref)]
    out_ref[...] = back_from(jnp.concatenate(spectra, axis=0), table_ref).reshape(out_ref.shape)
    store_parts(lambda j: out_ref[groups + j], lambda j: out_ref[j], parts)
    spread = jnp.broadcast_to(skip_ref[...][None, :], (block, gated_ref.shape[0])).T
    skipped_ref[...] = spread * gated_ref[...].astype(jnp.float32)


def far_kernel(table_ref, taps_ref, sums_ref, other_ref, came_ref, across_ref, *refs):
    outs, (waves_ref, total_ref, own_ref) = refs[:-3], refs[-3:]
    groups, rows, full = sums_ref.shape
    blocks = [came_ref[:rows, :]]
    blocks += [across_ref[at * rows : (at + 1) * rows, :] for at in range(groups, 2 * groups - 1)]
    store_waves(blocks, table_ref, [waves_ref])
    products(waves_ref, taps_ref, groups, total_ref, sums_ref)
    total = total_ref[...].reshape(groups * rows, full)
    own_ref[...] = back_from(total, table_ref).reshape(own_ref.shape)

    def other(j):
        return other_ref[j] + across_ref[span(j, rows), :].astype(jnp.float32)

    store_parts(lambda j: own_ref[j], other, outs)


def join_kernel(*refs):
    parts, out_ref = refs[:-1][::-1], refs[-1]
    groups = len(parts)
    _, group = place()
    rows = parts[0].shape[0] // HALVES
    for k, part_ref in enumerate(parts):
        for half in range(HALVES):
            out_ref[span(half * groups + (group ^ k), rows), :] = part_ref[
                half * rows : (half + 1) * rows, :
            ]


def copy_kernel(in_ref, out_ref):
    out_ref[...] = in_ref[...]


def final_kernel(queries_ref, skipped_ref, convolved_ref, out_ref):
    total = convolved_ref[...].astype(jnp.float32) + skipped_ref[...]
    out_ref[...] = (queries_ref[...].astype(jnp.float32) * total).astype(jnp.bfloat16)


VMEM = pl.BlockSpec(memory_space=pltpu.VMEM)
HBM = pl.BlockSpec(memory_space=pltpu.HBM)


def call(kernel, outs, args, scratch=(), far=0):
    args = [
        pltpu.with_memory_space_constraint(arg, pltpu.HBM) if i < far else arg
        for i, arg in enumerate(args)
    ]
    return pl.pallas_call(
        kernel,
        out_shape=[jax.ShapeDtypeStruct(shape, dtype) for shape, dtype in outs],
        in_specs=[HBM if i < far else VMEM for i in range(len(args))],
        out_specs=[VMEM] * len(outs),
        scratch_shapes=list(scratch),
        compiler_params=pltpu.CompilerParams(vmem_limit_bytes=16 * 1024 * 1024),
    )(*args)


def per_device(queries, keys, values, filters, skip):
    channels, block = keys.shape
    shards = lax.axis_size(AXIS)
    groups = shards // HALVES
    rows = channels // shards
    chans = HALVES * rows
    full = 2 * block
    f32, bf16 = jnp.float32, jnp.bfloat16
    table = jnp.asarray(transform_table(block))
    swap = lambda x, k: lax.ppermute(x, AXIS, [(i, i ^ k) for i in range(shards)])
    whole = ((channels, block), bf16)
    group_part = ((chans, block), bf16)
    waves_of = ((groups, rows, full), f32)
    taps_of = lambda count: ((count, rows, full), f32)
    across_part = (((2 * groups - 1) * rows, block), bf16)
    outputs = ((shards, rows, block), f32)
    scratch = lambda *shapes: [pltpu.VMEM(*shape) for shape in shapes]

    near = (filters, skip, table, queries)
    own, skip, table, queries, gated, coarse, *sends = call(
        prepare_kernel,
        [(x.shape, x.dtype) for x in near]
        + [whole, across_part]
        + [group_part] * groups,
        (keys, values, *near),
        scratch(whole, whole) + [pltpu.SemaphoreType.DMA((6,))],
        6,
    )
    other = swap(coarse, groups)
    arrived = [swap(sends[k], k) if k else sends[k] for k in range(groups - 1, -1, -1)]
    (lead,) = call(
        lead_kernel,
        [across_part],
        (table, own, *arrived),
        scratch(taps_of(shards), waves_of, waves_of),
    )
    across = swap(lead, groups)
    *parts, taps, sums, other_out, skipped = call(
        near_kernel,
        [group_part] * groups
        + [taps_of(shards), waves_of, outputs, ((channels, block), f32)],
        (table, own, other, gated, skip, *arrived),
        scratch(taps_of(groups), waves_of, waves_of, waves_of),
    )

    def give_back(parts):
        returned = [swap(parts[k], k) if k else parts[k] for k in range(groups - 1, -1, -1)]
        return call(join_kernel, [whole], returned)[0]

    def late(across):
        return give_back(
            call(
                far_kernel,
                [group_part] * groups,
                (table, taps, sums, other_out, other, across),
                scratch(waves_of, waves_of, ((groups, rows, block), f32)),
            )
        )

    copy = lambda x: call(copy_kernel, [whole], (x,))[0]
    first = lax.axis_index(AXIS) < groups
    convolved = lax.cond(first, lambda: give_back(parts), lambda: copy(gated))
    convolved = lax.cond(
        first, lambda done, _: copy(done), lambda _, across: late(across), convolved, across
    )
    return call(final_kernel, [whole], (queries, skipped, convolved))[0]


def solution(mesh):
    placed = (
        P("tensor", AXIS),
        P("tensor", AXIS),
        P("tensor", AXIS),
        P(("tensor", AXIS), None),
        P("tensor"),
    )
    return jax.shard_map(
        per_device, mesh=mesh, in_specs=placed, out_specs=P("tensor", AXIS), check_vma=False
    )
```

```python
import jax
import jax.numpy as jnp
import ml_dtypes
import numpy as np
from jax import lax
from jax.experimental import pallas as pl
from jax.experimental.pallas import tpu as pltpu
from jax.sharding import PartitionSpec as P

AXIS = "context"
HALVES = 2


def transform_table(block):
    angles = np.pi * np.outer(np.arange(block), 2 * np.arange(block) + 1) / (2 * block)
    table = np.concatenate([np.cos(angles), -np.sin(angles)], axis=1)
    high = table.astype(ml_dtypes.bfloat16)
    low = (table - high.astype(np.float64)).astype(ml_dtypes.bfloat16)
    return np.concatenate([high, low], axis=0)


def dot(left, right, turned=False):
    dims = (((1,), (1 if turned else 0,)), ((), ()))
    return lax.dot_general(left, right, dims, preferred_element_type=jnp.float32)


def split(values):
    high = values.astype(jnp.bfloat16)
    return high, (values - high.astype(jnp.float32)).astype(jnp.bfloat16)


def partners(groups):
    return (groups - 1, *range(1, groups - 1), 0)


def in_order(refs):
    order = partners(len(refs))
    return [refs[order.index(k)] for k in range(len(refs))]


def place():
    index = lax.axis_index(AXIS)
    groups = lax.axis_size(AXIS) // HALVES
    return index // groups, lax.rem(index, groups)


def span(start, size):
    return pl.ds(pl.multiple_of(start * size, size), size)


def store_waves(blocks, table_ref, waves_refs):
    _, group = place()
    rows = waves_refs[0].shape[1]
    stacked = jnp.concatenate(blocks, axis=0)
    spectra = dot(jnp.concatenate([stacked, stacked], axis=1), table_ref[...])
    parts = len(waves_refs)
    for k in range(len(blocks) // parts):
        for i, ref in enumerate(waves_refs):
            at = (k * parts + i) * rows
            ref[group ^ k] = spectra[at : at + rows]


def store_taps(taps, table_ref, taps_ref):
    count, rows, full = taps_ref.shape
    block = full // 2
    high, low = split(jnp.concatenate(taps, axis=0))
    spectra = dot(jnp.concatenate([high, high], axis=1), table_ref[...]) + dot(
        low, table_ref[:block, :]
    )
    odd = lax.rem(lax.broadcasted_iota(jnp.int32, (rows, block), 1), 2)
    sign = 1.0 - 2.0 * odd.astype(jnp.float32)
    for m in range(count):
        now = spectra[m * rows : (m + 1) * rows]
        if m == 0:
            taps_ref[m] = now
            continue
        past = spectra[(m - 1) * rows : m * rows]
        taps_ref[m, :, :block] = now[:, :block] - sign * past[:, block:]
        taps_ref[m, :, block:] = now[:, block:] + sign * past[:, :block]


def back_from(spectra, table_ref):
    block = spectra.shape[1] // 2
    high, low = split(spectra)
    top, rest = table_ref[:block, :], table_ref[block:, :]
    total = dot(high, top, True) + dot(low, top, True) + dot(high, rest, True)
    return total * (1.0 / block)


def products(waves_ref, taps_ref, shift, out_ref, start=None):
    groups, rows, full = waves_ref.shape
    block = full // 2
    for at in range(0, rows, 8):
        part = slice(at, at + 8)
        waves = [waves_ref[b, part, :] for b in range(groups)]
        for j in range(groups):
            total = [None, None]
            if start is not None:
                total = [start[j, part, :block], start[j, part, block:]]
            for b in range(groups):
                if shift + j < b:
                    continue
                tap = taps_ref[shift + j - b, part, :]
                re, im = waves[b][:, :block], waves[b][:, block:]
                tap_re, tap_im = tap[:, :block], tap[:, block:]
                new = [re * tap_re - im * tap_im, re * tap_im + im * tap_re]
                total = [n if t is None else t + n for t, n in zip(total, new)]
            out_ref[j, part, :block] = total[0]
            out_ref[j, part, block:] = total[1]


def prepare_kernel(*refs):
    sources, targets, (gated_ref, coarse_ref) = refs[:6], refs[6:10], refs[10:12]
    sends, (keys_ref, values_ref, sem) = refs[12:-3], refs[-3:]
    near_ref, block = targets[0], gated_ref.shape[1]
    half, group = place()
    copies = [
        pltpu.make_async_copy(source, target, sem.at[i])
        for i, (source, target) in enumerate(zip(sources, (keys_ref, values_ref, *targets)))
    ]
    for copy in copies:
        copy.start()
    copies[0].wait()
    copies[1].wait()
    gated_ref[...] = (
        keys_ref[...].astype(jnp.float32) * values_ref[...].astype(jnp.float32)
    ).astype(jnp.bfloat16)
    groups = len(sends)
    rows = sends[0].shape[0] // HALVES
    for k, send_ref in enumerate(sends):
        for part in range(HALVES):
            send_ref[part * rows : (part + 1) * rows, :] = gated_ref[
                span(part * groups + (group ^ k), rows), :
            ]
    copies[2].wait()
    coarse_ref[:rows, :] = sends[0][span(1 - half, rows), :]
    for m in range(groups):
        parts = split(near_ref[:, m * block : (m + 1) * block])
        coarse_ref[(m + 1) * rows : (m + 2) * rows, :] = parts[0]
        at = (groups + 1 + m) * rows
        if at < coarse_ref.shape[0]:
            coarse_ref[at : at + rows, :] = parts[1]
    for copy in copies[3:]:
        copy.wait()


def lead_kernel(table_ref, own_ref, *refs):
    arrived, (out_ref, taps_ref, waves_ref, sums_ref) = in_order(refs[:-4]), refs[-4:]
    half, _ = place()
    groups, rows, full = waves_ref.shape
    block = full // 2

    @pl.when(half == 0)
    def _():
        for k, ref in enumerate(arrived[1:]):
            out_ref[(groups + k) * rows : (groups + k + 1) * rows, :] = ref[rows:, :]
        store_taps(
            [own_ref[:, m * block : (m + 1) * block] for m in range(taps_ref.shape[0])],
            table_ref,
            taps_ref,
        )
        store_waves([ref[:rows, :] for ref in arrived], table_ref, [waves_ref])
        products(waves_ref, taps_ref, groups, sums_ref)
        sums = sums_ref[...].reshape(groups * rows, full)
        out_ref[: groups * rows, :] = back_from(sums, table_ref).astype(jnp.bfloat16)


def store_parts(own, other, outs):
    half, group = place()
    rows = outs[0].shape[0] // HALVES
    for k, out_ref in enumerate(outs):
        out_ref[span(half, rows), :] = own(group ^ k).astype(jnp.bfloat16)
        out_ref[span(1 - half, rows), :] = other(group ^ k).astype(jnp.bfloat16)


def near_kernel(table_ref, own_ref, other_ref, gated_ref, skip_ref, *refs):
    groups = (len(refs) - 8) // 2
    arrived, parts = in_order(refs[:groups]), refs[groups : 2 * groups]
    taps_ref, sums_ref, out_ref, skipped_ref = refs[2 * groups : 2 * groups + 4]
    other_taps_ref, own_waves_ref, waves_ref, other_sums_ref = refs[2 * groups + 4 :]
    half, _ = place()
    _, rows, full = sums_ref.shape
    block = full // 2
    store_taps(
        [own_ref[:, m * block : (m + 1) * block] for m in range(taps_ref.shape[0])],
        table_ref,
        taps_ref,
    )
    other_taps = []
    for m in range(groups):
        tap = other_ref[(m + 1) * rows : (m + 2) * rows, :].astype(jnp.float32)
        at = (groups + 1 + m) * rows
        if at < other_ref.shape[0]:
            tap = tap + other_ref[at : at + rows, :].astype(jnp.float32)
        other_taps.append(tap)
    store_taps(other_taps, table_ref, other_taps_ref)
    blocks = []
    for ref in arrived:
        blocks += [ref[span(half, rows), :], ref[span(1 - half, rows), :]]
    store_waves(blocks, table_ref, [own_waves_ref, waves_ref])
    products(own_waves_ref, taps_ref, 0, sums_ref)
    products(waves_ref, other_taps_ref, 0, other_sums_ref)
    spectra = [ref[...].reshape(groups * rows, full) for ref in (other_sums_ref, sums_ref)]
    out_ref[...] = back_from(jnp.concatenate(spectra, axis=0), table_ref).reshape(out_ref.shape)
    store_parts(lambda j: out_ref[groups + j], lambda j: out_ref[j], parts)
    spread = jnp.broadcast_to(skip_ref[...][None, :], (block, gated_ref.shape[0])).T
    skipped_ref[...] = spread * gated_ref[...].astype(jnp.float32)


def far_kernel(table_ref, taps_ref, sums_ref, other_ref, came_ref, across_ref, *refs):
    outs, (waves_ref, total_ref, own_ref) = refs[:-3], refs[-3:]
    groups, rows, full = sums_ref.shape
    blocks = [came_ref[:rows, :]]
    blocks += [across_ref[at * rows : (at + 1) * rows, :] for at in range(groups, 2 * groups - 1)]
    store_waves(blocks, table_ref, [waves_ref])
    products(waves_ref, taps_ref, groups, total_ref, sums_ref)
    total = total_ref[...].reshape(groups * rows, full)
    own_ref[...] = back_from(total, table_ref).reshape(own_ref.shape)

    def other(j):
        return other_ref[j] + across_ref[span(j, rows), :].astype(jnp.float32)

    store_parts(lambda j: own_ref[j], other, outs)


def join_kernel(*refs):
    parts, out_ref = in_order(refs[:-1]), refs[-1]
    groups = len(parts)
    _, group = place()
    rows = parts[0].shape[0] // HALVES
    for k, part_ref in enumerate(parts):
        for half in range(HALVES):
            out_ref[span(half * groups + (group ^ k), rows), :] = part_ref[
                half * rows : (half + 1) * rows, :
            ]


def copy_kernel(in_ref, out_ref):
    out_ref[...] = in_ref[...]


def final_kernel(queries_ref, skipped_ref, convolved_ref, out_ref):
    total = convolved_ref[...].astype(jnp.float32) + skipped_ref[...]
    out_ref[...] = (queries_ref[...].astype(jnp.float32) * total).astype(jnp.bfloat16)


VMEM = pl.BlockSpec(memory_space=pltpu.VMEM)
HBM = pl.BlockSpec(memory_space=pltpu.HBM)


def call(kernel, outs, args, scratch=(), far=0):
    args = [
        pltpu.with_memory_space_constraint(arg, pltpu.HBM) if i < far else arg
        for i, arg in enumerate(args)
    ]
    return pl.pallas_call(
        kernel,
        out_shape=[jax.ShapeDtypeStruct(shape, dtype) for shape, dtype in outs],
        in_specs=[HBM if i < far else VMEM for i in range(len(args))],
        out_specs=[VMEM] * len(outs),
        scratch_shapes=list(scratch),
        compiler_params=pltpu.CompilerParams(vmem_limit_bytes=16 * 1024 * 1024),
    )(*args)


def per_device(queries, keys, values, filters, skip):
    channels, block = keys.shape
    shards = lax.axis_size(AXIS)
    groups = shards // HALVES
    rows = channels // shards
    chans = HALVES * rows
    full = 2 * block
    f32, bf16 = jnp.float32, jnp.bfloat16
    table = jnp.asarray(transform_table(block))
    swap = lambda x, k: lax.ppermute(x, AXIS, [(i, i ^ k) for i in range(shards)])
    whole = ((channels, block), bf16)
    group_part = ((chans, block), bf16)
    waves_of = ((groups, rows, full), f32)
    taps_of = lambda count: ((count, rows, full), f32)
    across_part = (((2 * groups - 1) * rows, block), bf16)
    outputs = ((shards, rows, block), f32)
    scratch = lambda *shapes: [pltpu.VMEM(*shape) for shape in shapes]

    near = (filters, skip, table, queries)
    own, skip, table, queries, gated, coarse, *sends = call(
        prepare_kernel,
        [(x.shape, x.dtype) for x in near]
        + [whole, across_part]
        + [group_part] * groups,
        (keys, values, *near),
        scratch(whole, whole) + [pltpu.SemaphoreType.DMA((6,))],
        6,
    )
    other = swap(coarse, groups)
    arrived = [swap(sends[k], k) if k else sends[k] for k in partners(groups)]
    (lead,) = call(
        lead_kernel,
        [across_part],
        (table, own, *arrived),
        scratch(taps_of(shards), waves_of, waves_of),
    )
    across = swap(lead, groups)
    *parts, taps, sums, other_out, skipped = call(
        near_kernel,
        [group_part] * groups
        + [taps_of(shards), waves_of, outputs, ((channels, block), f32)],
        (table, own, other, gated, skip, *arrived),
        scratch(taps_of(groups), waves_of, waves_of, waves_of),
    )

    def give_back(parts):
        returned = [swap(parts[k], k) if k else parts[k] for k in partners(groups)]
        return call(join_kernel, [whole], returned)[0]

    def late(across):
        return give_back(
            call(
                far_kernel,
                [group_part] * groups,
                (table, taps, sums, other_out, other, across),
                scratch(waves_of, waves_of, ((groups, rows, block), f32)),
            )
        )

    copy = lambda x: call(copy_kernel, [whole], (x,))[0]
    first = lax.axis_index(AXIS) < groups
    convolved = lax.cond(first, lambda: give_back(parts), lambda: copy(gated))
    convolved = lax.cond(
        first, lambda done, _: copy(done), lambda _, across: late(across), convolved, across
    )
    return call(final_kernel, [whole], (queries, skipped, convolved))[0]


def solution(mesh):
    placed = (
        P("tensor", AXIS),
        P("tensor", AXIS),
        P("tensor", AXIS),
        P(("tensor", AXIS), None),
        P("tensor"),
    )
    return jax.shard_map(
        per_device, mesh=mesh, in_specs=placed, out_specs=P("tensor", AXIS), check_vma=False
    )
```

```python
import jax
import jax.numpy as jnp
import ml_dtypes
import numpy as np
from jax import lax
from jax.experimental import pallas as pl
from jax.experimental.pallas import tpu as pltpu
from jax.sharding import PartitionSpec as P

AXIS = "context"
HALVES = 2


def transform_table(block):
    angles = np.pi * np.outer(np.arange(block), 2 * np.arange(block) + 1) / (2 * block)
    table = np.concatenate([np.cos(angles), -np.sin(angles)], axis=1)
    high = table.astype(ml_dtypes.bfloat16)
    low = (table - high.astype(np.float64)).astype(ml_dtypes.bfloat16)
    return np.concatenate([high, low], axis=0)


def dot(left, right, turned=False):
    dims = (((1,), (1 if turned else 0,)), ((), ()))
    return lax.dot_general(left, right, dims, preferred_element_type=jnp.float32)


def split(values):
    high = values.astype(jnp.bfloat16)
    return high, (values - high.astype(jnp.float32)).astype(jnp.bfloat16)


def partners(groups):
    return (groups - 1, *range(1, groups - 1), 0)


def in_order(refs):
    order = partners(len(refs))
    return [refs[order.index(k)] for k in range(len(refs))]


def place():
    index = lax.axis_index(AXIS)
    groups = lax.axis_size(AXIS) // HALVES
    return index // groups, lax.rem(index, groups)


def span(start, size):
    return pl.ds(pl.multiple_of(start * size, size), size)


def store_waves(blocks, table_ref, waves_refs):
    _, group = place()
    rows = waves_refs[0].shape[1]
    stacked = jnp.concatenate(blocks, axis=0)
    spectra = dot(jnp.concatenate([stacked, stacked], axis=1), table_ref[...])
    parts = len(waves_refs)
    for k in range(len(blocks) // parts):
        for i, ref in enumerate(waves_refs):
            at = (k * parts + i) * rows
            ref[group ^ k] = spectra[at : at + rows]


def store_taps(taps, table_ref, taps_ref):
    count, rows, full = taps_ref.shape
    block = full // 2
    high, low = split(jnp.concatenate(taps, axis=0))
    spectra = dot(jnp.concatenate([high, high], axis=1), table_ref[...]) + dot(
        low, table_ref[:block, :]
    )
    odd = lax.rem(lax.broadcasted_iota(jnp.int32, (rows, block), 1), 2)
    sign = 1.0 - 2.0 * odd.astype(jnp.float32)
    for m in range(count):
        now = spectra[m * rows : (m + 1) * rows]
        if m == 0:
            taps_ref[m] = now
            continue
        past = spectra[(m - 1) * rows : m * rows]
        taps_ref[m, :, :block] = now[:, :block] - sign * past[:, block:]
        taps_ref[m, :, block:] = now[:, block:] + sign * past[:, :block]


def back_from(spectra, table_ref):
    block = spectra.shape[1] // 2
    high, low = split(spectra)
    top, rest = table_ref[:block, :], table_ref[block:, :]
    total = dot(high, top, True) + dot(low, top, True) + dot(high, rest, True)
    return total * (1.0 / block)


def products(waves_ref, taps_ref, shift, out_ref, start=None):
    groups, rows, full = waves_ref.shape
    block = full // 2
    for at in range(0, rows, 8):
        part = slice(at, at + 8)
        waves = [waves_ref[b, part, :] for b in range(groups)]
        for j in range(groups):
            total = [None, None]
            if start is not None:
                total = [start[j, part, :block], start[j, part, block:]]
            for b in range(groups):
                if shift + j < b:
                    continue
                tap = taps_ref[shift + j - b, part, :]
                re, im = waves[b][:, :block], waves[b][:, block:]
                tap_re, tap_im = tap[:, :block], tap[:, block:]
                new = [re * tap_re - im * tap_im, re * tap_im + im * tap_re]
                total = [n if t is None else t + n for t, n in zip(total, new)]
            out_ref[j, part, :block] = total[0]
            out_ref[j, part, block:] = total[1]


def gate_kernel(*refs):
    sources, targets, gated_ref = refs[:4], refs[4:6], refs[6]
    sends, (keys_ref, values_ref, sem) = refs[7:-3], refs[-3:]
    copies = [
        pltpu.make_async_copy(source, target, sem.at[i])
        for i, (source, target) in enumerate(zip(sources, (keys_ref, values_ref, *targets)))
    ]
    for copy in copies:
        copy.start()
    copies[0].wait()
    copies[1].wait()
    gated_ref[...] = (
        keys_ref[...].astype(jnp.float32) * values_ref[...].astype(jnp.float32)
    ).astype(jnp.bfloat16)
    groups = len(sends)
    _, group = place()
    rows = sends[0].shape[0] // HALVES
    for k, send_ref in enumerate(sends):
        for part in range(HALVES):
            send_ref[part * rows : (part + 1) * rows, :] = gated_ref[
                span(part * groups + (group ^ k), rows), :
            ]
    for copy in copies[2:]:
        copy.wait()


def coarse_kernel(near_ref, stays_ref, coarse_ref):
    half, _ = place()
    chans, block = stays_ref.shape
    rows = chans // HALVES
    groups = near_ref.shape[1] // block // HALVES
    coarse_ref[:rows, :] = stays_ref[span(1 - half, rows), :]
    for m in range(groups):
        parts = split(near_ref[:, m * block : (m + 1) * block])
        coarse_ref[(m + 1) * rows : (m + 2) * rows, :] = parts[0]
        at = (groups + 1 + m) * rows
        if at < coarse_ref.shape[0]:
            coarse_ref[at : at + rows, :] = parts[1]


def lead_kernel(table_ref, own_ref, *refs):
    arrived, (out_ref, taps_ref, waves_ref, sums_ref) = in_order(refs[:-4]), refs[-4:]
    half, _ = place()
    groups, rows, full = waves_ref.shape
    block = full // 2

    @pl.when(half == 0)
    def _():
        for k, ref in enumerate(arrived[1:]):
            out_ref[(groups + k) * rows : (groups + k + 1) * rows, :] = ref[rows:, :]
        store_taps(
            [own_ref[:, m * block : (m + 1) * block] for m in range(taps_ref.shape[0])],
            table_ref,
            taps_ref,
        )
        store_waves([ref[:rows, :] for ref in arrived], table_ref, [waves_ref])
        products(waves_ref, taps_ref, groups, sums_ref)
        sums = sums_ref[...].reshape(groups * rows, full)
        out_ref[: groups * rows, :] = back_from(sums, table_ref).astype(jnp.bfloat16)


def store_parts(own, other, outs):
    half, group = place()
    rows = outs[0].shape[0] // HALVES
    for k, out_ref in enumerate(outs):
        out_ref[span(half, rows), :] = own(group ^ k).astype(jnp.bfloat16)
        out_ref[span(1 - half, rows), :] = other(group ^ k).astype(jnp.bfloat16)


def near_kernel(table_ref, own_ref, other_ref, gated_ref, skip_ref, *refs):
    groups = (len(refs) - 8) // 2
    arrived, parts = in_order(refs[:groups]), refs[groups : 2 * groups]
    taps_ref, sums_ref, out_ref, skipped_ref = refs[2 * groups : 2 * groups + 4]
    other_taps_ref, own_waves_ref, waves_ref, other_sums_ref = refs[2 * groups + 4 :]
    half, _ = place()
    _, rows, full = sums_ref.shape
    block = full // 2
    store_taps(
        [own_ref[:, m * block : (m + 1) * block] for m in range(taps_ref.shape[0])],
        table_ref,
        taps_ref,
    )
    other_taps = []
    for m in range(groups):
        tap = other_ref[(m + 1) * rows : (m + 2) * rows, :].astype(jnp.float32)
        at = (groups + 1 + m) * rows
        if at < other_ref.shape[0]:
            tap = tap + other_ref[at : at + rows, :].astype(jnp.float32)
        other_taps.append(tap)
    store_taps(other_taps, table_ref, other_taps_ref)
    blocks = []
    for ref in arrived:
        blocks += [ref[span(half, rows), :], ref[span(1 - half, rows), :]]
    store_waves(blocks, table_ref, [own_waves_ref, waves_ref])
    products(own_waves_ref, taps_ref, 0, sums_ref)
    products(waves_ref, other_taps_ref, 0, other_sums_ref)
    spectra = [ref[...].reshape(groups * rows, full) for ref in (other_sums_ref, sums_ref)]
    out_ref[...] = back_from(jnp.concatenate(spectra, axis=0), table_ref).reshape(out_ref.shape)
    store_parts(lambda j: out_ref[groups + j], lambda j: out_ref[j], parts)
    spread = jnp.broadcast_to(skip_ref[...][None, :], (block, gated_ref.shape[0])).T
    skipped_ref[...] = spread * gated_ref[...].astype(jnp.float32)


def far_kernel(table_ref, taps_ref, sums_ref, other_ref, came_ref, across_ref, *refs):
    outs, (waves_ref, total_ref, own_ref) = refs[:-3], refs[-3:]
    groups, rows, full = sums_ref.shape
    blocks = [came_ref[:rows, :]]
    blocks += [across_ref[at * rows : (at + 1) * rows, :] for at in range(groups, 2 * groups - 1)]
    store_waves(blocks, table_ref, [waves_ref])
    products(waves_ref, taps_ref, groups, total_ref, sums_ref)
    total = total_ref[...].reshape(groups * rows, full)
    own_ref[...] = back_from(total, table_ref).reshape(own_ref.shape)

    def other(j):
        return other_ref[j] + across_ref[span(j, rows), :].astype(jnp.float32)

    store_parts(lambda j: own_ref[j], other, outs)


def join_kernel(*refs):
    parts, out_ref = in_order(refs[:-1]), refs[-1]
    groups = len(parts)
    _, group = place()
    rows = parts[0].shape[0] // HALVES
    for k, part_ref in enumerate(parts):
        for half in range(HALVES):
            out_ref[span(half * groups + (group ^ k), rows), :] = part_ref[
                half * rows : (half + 1) * rows, :
            ]


def copy_kernel(in_ref, out_ref):
    out_ref[...] = in_ref[...]


def final_kernel(queries_ref, skipped_ref, convolved_ref, out_ref):
    total = convolved_ref[...].astype(jnp.float32) + skipped_ref[...]
    out_ref[...] = (queries_ref[...].astype(jnp.float32) * total).astype(jnp.bfloat16)


VMEM = pl.BlockSpec(memory_space=pltpu.VMEM)
HBM = pl.BlockSpec(memory_space=pltpu.HBM)


def call(kernel, outs, args, scratch=(), far=0):
    args = [
        pltpu.with_memory_space_constraint(arg, pltpu.HBM) if i < far else arg
        for i, arg in enumerate(args)
    ]
    return pl.pallas_call(
        kernel,
        out_shape=[jax.ShapeDtypeStruct(shape, dtype) for shape, dtype in outs],
        in_specs=[HBM if i < far else VMEM for i in range(len(args))],
        out_specs=[VMEM] * len(outs),
        scratch_shapes=list(scratch),
        compiler_params=pltpu.CompilerParams(vmem_limit_bytes=16 * 1024 * 1024),
    )(*args)


def per_device(queries, keys, values, filters, skip):
    channels, block = keys.shape
    shards = lax.axis_size(AXIS)
    groups = shards // HALVES
    rows = channels // shards
    chans = HALVES * rows
    full = 2 * block
    f32, bf16 = jnp.float32, jnp.bfloat16
    table = jnp.asarray(transform_table(block))
    swap = lambda x, k: lax.ppermute(x, AXIS, [(i, i ^ k) for i in range(shards)])
    whole = ((channels, block), bf16)
    group_part = ((chans, block), bf16)
    waves_of = ((groups, rows, full), f32)
    taps_of = lambda count: ((count, rows, full), f32)
    across_part = (((2 * groups - 1) * rows, block), bf16)
    outputs = ((shards, rows, block), f32)
    scratch = lambda *shapes: [pltpu.VMEM(*shape) for shape in shapes]

    queries, skip, gated, *sends = call(
        gate_kernel,
        [whole, (skip.shape, f32), whole] + [group_part] * groups,
        (keys, values, queries, skip),
        scratch(whole, whole) + [pltpu.SemaphoreType.DMA((4,))],
        4,
    )
    own = filters
    (coarse,) = call(coarse_kernel, [across_part], (own, sends[0]))
    other = swap(coarse, groups)
    arrived = [swap(sends[k], k) if k else sends[k] for k in partners(groups)]
    (lead,) = call(
        lead_kernel,
        [across_part],
        (table, own, *arrived),
        scratch(taps_of(shards), waves_of, waves_of),
    )
    across = swap(lead, groups)
    *parts, taps, sums, other_out, skipped = call(
        near_kernel,
        [group_part] * groups
        + [taps_of(shards), waves_of, outputs, ((channels, block), f32)],
        (table, own, other, gated, skip, *arrived),
        scratch(taps_of(groups), waves_of, waves_of, waves_of),
    )

    def give_back(parts):
        returned = [swap(parts[k], k) if k else parts[k] for k in partners(groups)]
        return call(join_kernel, [whole], returned)[0]

    def late(across):
        return give_back(
            call(
                far_kernel,
                [group_part] * groups,
                (table, taps, sums, other_out, other, across),
                scratch(waves_of, waves_of, ((groups, rows, block), f32)),
            )
        )

    copy = lambda x: call(copy_kernel, [whole], (x,))[0]
    first = lax.axis_index(AXIS) < groups
    convolved = lax.cond(first, lambda: give_back(parts), lambda: copy(gated))
    convolved = lax.cond(
        first, lambda done, _: copy(done), lambda _, across: late(across), convolved, across
    )
    return call(final_kernel, [whole], (queries, skipped, convolved))[0]


def solution(mesh):
    placed = (
        P("tensor", AXIS),
        P("tensor", AXIS),
        P("tensor", AXIS),
        P(("tensor", AXIS), None),
        P("tensor"),
    )
    return jax.shard_map(
        per_device, mesh=mesh, in_specs=placed, out_specs=P("tensor", AXIS), check_vma=False
    )
```

```python
import jax
import jax.numpy as jnp
import ml_dtypes
import numpy as np
from jax import lax
from jax.experimental import pallas as pl
from jax.experimental.pallas import tpu as pltpu
from jax.sharding import PartitionSpec as P

AXIS = "context"
HALVES = 2


def transform_table(block):
    angles = np.pi * np.outer(np.arange(block), 2 * np.arange(block) + 1) / (2 * block)
    table = np.concatenate([np.cos(angles), -np.sin(angles)], axis=1)
    high = table.astype(ml_dtypes.bfloat16)
    low = (table - high.astype(np.float64)).astype(ml_dtypes.bfloat16)
    return np.concatenate([high, low], axis=0)


def dot(left, right, turned=False):
    dims = (((1,), (1 if turned else 0,)), ((), ()))
    return lax.dot_general(left, right, dims, preferred_element_type=jnp.float32)


def split(values):
    high = values.astype(jnp.bfloat16)
    return high, (values - high.astype(jnp.float32)).astype(jnp.bfloat16)


def partners(groups):
    return (groups - 1, *range(1, groups - 1), 0)


def in_order(refs):
    order = partners(len(refs))
    return [refs[order.index(k)] for k in range(len(refs))]


def place():
    index = lax.axis_index(AXIS)
    groups = lax.axis_size(AXIS) // HALVES
    return index // groups, lax.rem(index, groups)


def span(start, size):
    return pl.ds(pl.multiple_of(start * size, size), size)


def store_waves(blocks, table_ref, waves_refs):
    _, group = place()
    rows = waves_refs[0].shape[1]
    stacked = jnp.concatenate(blocks, axis=0)
    spectra = dot(jnp.concatenate([stacked, stacked], axis=1), table_ref[...])
    parts = len(waves_refs)
    for k in range(len(blocks) // parts):
        for i, ref in enumerate(waves_refs):
            at = (k * parts + i) * rows
            ref[group ^ k] = spectra[at : at + rows]


def store_taps(taps, table_ref, taps_ref):
    count, rows, full = taps_ref.shape
    block = full // 2
    high, low = split(jnp.concatenate(taps, axis=0))
    spectra = dot(jnp.concatenate([high, high], axis=1), table_ref[...]) + dot(
        low, table_ref[:block, :]
    )
    odd = lax.rem(lax.broadcasted_iota(jnp.int32, (rows, block), 1), 2)
    sign = 1.0 - 2.0 * odd.astype(jnp.float32)
    for m in range(count):
        now = spectra[m * rows : (m + 1) * rows]
        if m == 0:
            taps_ref[m] = now
            continue
        past = spectra[(m - 1) * rows : m * rows]
        taps_ref[m, :, :block] = now[:, :block] - sign * past[:, block:]
        taps_ref[m, :, block:] = now[:, block:] + sign * past[:, :block]


def back_from(spectra, table_ref):
    block = spectra.shape[1] // 2
    high, low = split(spectra)
    both = dot(jnp.concatenate([high, low], axis=0), table_ref[...], True)
    count = len(high)
    total = both[:count, :block] + both[count:, :block] + both[:count, block:]
    return total * (1.0 / block)


def products(waves_ref, taps_ref, shift, out_ref, start=None):
    groups, rows, full = waves_ref.shape
    block = full // 2
    for at in range(0, rows, 8):
        part = slice(at, at + 8)
        waves = [waves_ref[b, part, :] for b in range(groups)]
        for j in range(groups):
            total = [None, None]
            if start is not None:
                total = [start[j, part, :block], start[j, part, block:]]
            for b in range(groups):
                if shift + j < b:
                    continue
                tap = taps_ref[shift + j - b, part, :]
                re, im = waves[b][:, :block], waves[b][:, block:]
                tap_re, tap_im = tap[:, :block], tap[:, block:]
                new = [re * tap_re - im * tap_im, re * tap_im + im * tap_re]
                total = [n if t is None else t + n for t, n in zip(total, new)]
            out_ref[j, part, :block] = total[0]
            out_ref[j, part, block:] = total[1]


def gate_kernel(*refs):
    sources, targets, gated_ref = refs[:4], refs[4:6], refs[6]
    sends, (keys_ref, values_ref, sem) = refs[7:-3], refs[-3:]
    copies = [
        pltpu.make_async_copy(source, target, sem.at[i])
        for i, (source, target) in enumerate(zip(sources, (keys_ref, values_ref, *targets)))
    ]
    for copy in copies:
        copy.start()
    copies[0].wait()
    copies[1].wait()
    gated_ref[...] = (
        keys_ref[...].astype(jnp.float32) * values_ref[...].astype(jnp.float32)
    ).astype(jnp.bfloat16)
    groups = len(sends)
    _, group = place()
    rows = sends[0].shape[0] // HALVES
    for k, send_ref in enumerate(sends):
        for part in range(HALVES):
            send_ref[part * rows : (part + 1) * rows, :] = gated_ref[
                span(part * groups + (group ^ k), rows), :
            ]
    for copy in copies[2:]:
        copy.wait()


def coarse_kernel(near_ref, stays_ref, coarse_ref):
    half, _ = place()
    chans, block = stays_ref.shape
    rows = chans // HALVES
    groups = near_ref.shape[1] // block // HALVES
    coarse_ref[:rows, :] = stays_ref[span(1 - half, rows), :]
    for m in range(groups):
        parts = split(near_ref[:, m * block : (m + 1) * block])
        coarse_ref[(m + 1) * rows : (m + 2) * rows, :] = parts[0]
        at = (groups + 1 + m) * rows
        if at < coarse_ref.shape[0]:
            coarse_ref[at : at + rows, :] = parts[1]


def lead_kernel(table_ref, own_ref, *refs):
    arrived, (out_ref, taps_ref, waves_ref, sums_ref) = in_order(refs[:-4]), refs[-4:]
    half, _ = place()
    groups, rows, full = waves_ref.shape
    block = full // 2

    @pl.when(half == 0)
    def _():
        for k, ref in enumerate(arrived[1:]):
            out_ref[(groups + k) * rows : (groups + k + 1) * rows, :] = ref[rows:, :]
        store_taps(
            [own_ref[:, m * block : (m + 1) * block] for m in range(taps_ref.shape[0])],
            table_ref,
            taps_ref,
        )
        store_waves([ref[:rows, :] for ref in arrived], table_ref, [waves_ref])
        products(waves_ref, taps_ref, groups, sums_ref)
        sums = sums_ref[...].reshape(groups * rows, full)
        out_ref[: groups * rows, :] = back_from(sums, table_ref).astype(jnp.bfloat16)


def store_parts(own, other, outs):
    half, group = place()
    rows = outs[0].shape[0] // HALVES
    for k, out_ref in enumerate(outs):
        out_ref[span(half, rows), :] = own(group ^ k).astype(jnp.bfloat16)
        out_ref[span(1 - half, rows), :] = other(group ^ k).astype(jnp.bfloat16)


def near_kernel(table_ref, own_ref, other_ref, gated_ref, skip_ref, *refs):
    groups = (len(refs) - 8) // 2
    arrived, parts = in_order(refs[:groups]), refs[groups : 2 * groups]
    taps_ref, sums_ref, out_ref, skipped_ref = refs[2 * groups : 2 * groups + 4]
    other_taps_ref, own_waves_ref, waves_ref, other_sums_ref = refs[2 * groups + 4 :]
    half, _ = place()
    _, rows, full = sums_ref.shape
    block = full // 2
    store_taps(
        [own_ref[:, m * block : (m + 1) * block] for m in range(taps_ref.shape[0])],
        table_ref,
        taps_ref,
    )
    other_taps = []
    for m in range(groups):
        tap = other_ref[(m + 1) * rows : (m + 2) * rows, :].astype(jnp.float32)
        at = (groups + 1 + m) * rows
        if at < other_ref.shape[0]:
            tap = tap + other_ref[at : at + rows, :].astype(jnp.float32)
        other_taps.append(tap)
    store_taps(other_taps, table_ref, other_taps_ref)
    blocks = []
    for ref in arrived:
        blocks += [ref[span(half, rows), :], ref[span(1 - half, rows), :]]
    store_waves(blocks, table_ref, [own_waves_ref, waves_ref])
    products(own_waves_ref, taps_ref, 0, sums_ref)
    products(waves_ref, other_taps_ref, 0, other_sums_ref)
    spectra = [ref[...].reshape(groups * rows, full) for ref in (other_sums_ref, sums_ref)]
    out_ref[...] = back_from(jnp.concatenate(spectra, axis=0), table_ref).reshape(out_ref.shape)
    store_parts(lambda j: out_ref[groups + j], lambda j: out_ref[j], parts)
    spread = jnp.broadcast_to(skip_ref[...][None, :], (block, gated_ref.shape[0])).T
    skipped_ref[...] = spread * gated_ref[...].astype(jnp.float32)


def far_kernel(table_ref, taps_ref, sums_ref, other_ref, came_ref, across_ref, *refs):
    outs, (waves_ref, total_ref, own_ref) = refs[:-3], refs[-3:]
    groups, rows, full = sums_ref.shape
    blocks = [came_ref[:rows, :]]
    blocks += [across_ref[at * rows : (at + 1) * rows, :] for at in range(groups, 2 * groups - 1)]
    store_waves(blocks, table_ref, [waves_ref])
    products(waves_ref, taps_ref, groups, total_ref, sums_ref)
    total = total_ref[...].reshape(groups * rows, full)
    own_ref[...] = back_from(total, table_ref).reshape(own_ref.shape)

    def other(j):
        return other_ref[j] + across_ref[span(j, rows), :].astype(jnp.float32)

    store_parts(lambda j: own_ref[j], other, outs)


def join_kernel(*refs):
    parts, out_ref = in_order(refs[:-1]), refs[-1]
    groups = len(parts)
    _, group = place()
    rows = parts[0].shape[0] // HALVES
    for k, part_ref in enumerate(parts):
        for half in range(HALVES):
            out_ref[span(half * groups + (group ^ k), rows), :] = part_ref[
                half * rows : (half + 1) * rows, :
            ]


def copy_kernel(in_ref, out_ref):
    out_ref[...] = in_ref[...]


def final_kernel(queries_ref, skipped_ref, convolved_ref, out_ref):
    total = convolved_ref[...].astype(jnp.float32) + skipped_ref[...]
    out_ref[...] = (queries_ref[...].astype(jnp.float32) * total).astype(jnp.bfloat16)


VMEM = pl.BlockSpec(memory_space=pltpu.VMEM)
HBM = pl.BlockSpec(memory_space=pltpu.HBM)


def call(kernel, outs, args, scratch=(), far=0):
    args = [
        pltpu.with_memory_space_constraint(arg, pltpu.HBM) if i < far else arg
        for i, arg in enumerate(args)
    ]
    return pl.pallas_call(
        kernel,
        out_shape=[jax.ShapeDtypeStruct(shape, dtype) for shape, dtype in outs],
        in_specs=[HBM if i < far else VMEM for i in range(len(args))],
        out_specs=[VMEM] * len(outs),
        scratch_shapes=list(scratch),
        compiler_params=pltpu.CompilerParams(vmem_limit_bytes=16 * 1024 * 1024),
    )(*args)


def per_device(queries, keys, values, filters, skip):
    channels, block = keys.shape
    shards = lax.axis_size(AXIS)
    groups = shards // HALVES
    rows = channels // shards
    chans = HALVES * rows
    full = 2 * block
    f32, bf16 = jnp.float32, jnp.bfloat16
    table = jnp.asarray(transform_table(block))
    swap = lambda x, k: lax.ppermute(x, AXIS, [(i, i ^ k) for i in range(shards)])
    whole = ((channels, block), bf16)
    group_part = ((chans, block), bf16)
    waves_of = ((groups, rows, full), f32)
    taps_of = lambda count: ((count, rows, full), f32)
    across_part = (((2 * groups - 1) * rows, block), bf16)
    outputs = ((shards, rows, block), f32)
    scratch = lambda *shapes: [pltpu.VMEM(*shape) for shape in shapes]

    queries, skip, gated, *sends = call(
        gate_kernel,
        [whole, (skip.shape, f32), whole] + [group_part] * groups,
        (keys, values, queries, skip),
        scratch(whole, whole) + [pltpu.SemaphoreType.DMA((4,))],
        4,
    )
    own = filters
    (coarse,) = call(coarse_kernel, [across_part], (own, sends[0]))
    other = swap(coarse, groups)
    arrived = [swap(sends[k], k) if k else sends[k] for k in partners(groups)]
    (lead,) = call(
        lead_kernel,
        [across_part],
        (table, own, *arrived),
        scratch(taps_of(shards), waves_of, waves_of),
    )
    across = swap(lead, groups)
    *parts, taps, sums, other_out, skipped = call(
        near_kernel,
        [group_part] * groups
        + [taps_of(shards), waves_of, outputs, ((channels, block), f32)],
        (table, own, other, gated, skip, *arrived),
        scratch(taps_of(groups), waves_of, waves_of, waves_of),
    )

    def give_back(parts):
        returned = [swap(parts[k], k) if k else parts[k] for k in partners(groups)]
        return call(join_kernel, [whole], returned)[0]

    def late(across):
        return give_back(
            call(
                far_kernel,
                [group_part] * groups,
                (table, taps, sums, other_out, other, across),
                scratch(waves_of, waves_of, ((groups, rows, block), f32)),
            )
        )

    copy = lambda x: call(copy_kernel, [whole], (x,))[0]
    first = lax.axis_index(AXIS) < groups
    convolved = lax.cond(first, lambda: give_back(parts), lambda: copy(gated))
    convolved = lax.cond(
        first, lambda done, _: copy(done), lambda _, across: late(across), convolved, across
    )
    return call(final_kernel, [whole], (queries, skipped, convolved))[0]


def solution(mesh):
    placed = (
        P("tensor", AXIS),
        P("tensor", AXIS),
        P("tensor", AXIS),
        P(("tensor", AXIS), None),
        P("tensor"),
    )
    return jax.shard_map(
        per_device, mesh=mesh, in_specs=placed, out_specs=P("tensor", AXIS), check_vma=False
    )
```

```python
import jax
import jax.numpy as jnp
import ml_dtypes
import numpy as np
from jax import lax
from jax.experimental import pallas as pl
from jax.experimental.pallas import tpu as pltpu
from jax.sharding import PartitionSpec as P

AXIS = "context"
HALVES = 2


def transform_table(block):
    angles = np.pi * np.outer(np.arange(block), 2 * np.arange(block) + 1) / (2 * block)
    table = np.concatenate([np.cos(angles), -np.sin(angles)], axis=1)
    high = table.astype(ml_dtypes.bfloat16)
    low = (table - high.astype(np.float64)).astype(ml_dtypes.bfloat16)
    return np.concatenate([high, low], axis=0)


def dot(left, right, turned=False):
    dims = (((1,), (1 if turned else 0,)), ((), ()))
    return lax.dot_general(left, right, dims, preferred_element_type=jnp.float32)


def split(values):
    high = values.astype(jnp.bfloat16)
    return high, (values - high.astype(jnp.float32)).astype(jnp.bfloat16)


def partners(groups):
    return (groups - 1, *range(1, groups - 1), 0)


def in_order(refs):
    order = partners(len(refs))
    return [refs[order.index(k)] for k in range(len(refs))]


def place():
    index = lax.axis_index(AXIS)
    groups = lax.axis_size(AXIS) // HALVES
    return index // groups, lax.rem(index, groups)


def span(start, size):
    return pl.ds(pl.multiple_of(start * size, size), size)


def store_waves(blocks, table_ref, waves_refs):
    _, group = place()
    rows = waves_refs[0].shape[1]
    stacked = jnp.concatenate(blocks, axis=0)
    spectra = dot(jnp.concatenate([stacked, stacked], axis=1), table_ref[...])
    parts = len(waves_refs)
    for k in range(len(blocks) // parts):
        for i, ref in enumerate(waves_refs):
            at = (k * parts + i) * rows
            ref[group ^ k] = spectra[at : at + rows]


def store_taps(taps, table_ref, taps_ref):
    count, rows, full = taps_ref.shape
    block = full // 2
    high, low = split(jnp.concatenate(taps, axis=0))
    spectra = dot(jnp.concatenate([high, high], axis=1), table_ref[...]) + dot(
        low, table_ref[:block, :]
    )
    odd = lax.rem(lax.broadcasted_iota(jnp.int32, (rows, block), 1), 2)
    sign = 1.0 - 2.0 * odd.astype(jnp.float32)
    for m in range(count):
        now = spectra[m * rows : (m + 1) * rows]
        if m == 0:
            taps_ref[m] = now
            continue
        past = spectra[(m - 1) * rows : m * rows]
        taps_ref[m, :, :block] = now[:, :block] - sign * past[:, block:]
        taps_ref[m, :, block:] = now[:, block:] + sign * past[:, :block]


def back_from(spectra, table_ref):
    block = spectra.shape[1] // 2
    high, low = split(spectra)
    top, rest = table_ref[:block, :], table_ref[block:, :]
    total = dot(high, top, True) + dot(low, top, True) + dot(high, rest, True)
    return total * (1.0 / block)


def products(waves_ref, taps_ref, shift, out_ref, start=None):
    groups, rows, full = waves_ref.shape
    block = full // 2
    for at in range(0, rows, 8):
        part = slice(at, at + 8)
        waves = [waves_ref[b, part, :] for b in range(groups)]
        for j in range(groups):
            total = [None, None]
            if start is not None:
                total = [start[j, part, :block], start[j, part, block:]]
            for b in range(groups):
                if shift + j < b:
                    continue
                tap = taps_ref[shift + j - b, part, :]
                re, im = waves[b][:, :block], waves[b][:, block:]
                tap_re, tap_im = tap[:, :block], tap[:, block:]
                new = [re * tap_re - im * tap_im, re * tap_im + im * tap_re]
                total = [n if t is None else t + n for t, n in zip(total, new)]
            out_ref[j, part, :block] = total[0]
            out_ref[j, part, block:] = total[1]


def gate_kernel(*refs):
    sources, targets, gated_ref = refs[:4], refs[4:6], refs[6]
    sends, (keys_ref, values_ref, sem) = refs[7:-3], refs[-3:]
    copies = [
        pltpu.make_async_copy(source, target, sem.at[i])
        for i, (source, target) in enumerate(zip(sources, (keys_ref, values_ref, *targets)))
    ]
    for copy in copies:
        copy.start()
    copies[0].wait()
    copies[1].wait()
    gated_ref[...] = (
        keys_ref[...].astype(jnp.float32) * values_ref[...].astype(jnp.float32)
    ).astype(jnp.bfloat16)
    groups = len(sends)
    _, group = place()
    rows = sends[0].shape[0] // HALVES
    for k, send_ref in enumerate(sends):
        for part in range(HALVES):
            send_ref[part * rows : (part + 1) * rows, :] = gated_ref[
                span(part * groups + (group ^ k), rows), :
            ]
    for copy in copies[2:]:
        copy.wait()


def coarse_kernel(near_ref, stays_ref, coarse_ref):
    half, _ = place()
    chans, block = stays_ref.shape
    rows = chans // HALVES
    groups = near_ref.shape[1] // block // HALVES
    coarse_ref[:rows, :] = stays_ref[span(1 - half, rows), :]
    for m in range(groups):
        coarse_ref[(m + 1) * rows : (m + 2) * rows, :] = near_ref[
            :, m * block : (m + 1) * block
        ].astype(jnp.bfloat16)


def lead_kernel(table_ref, own_ref, *refs):
    arrived, (out_ref, taps_ref, waves_ref, sums_ref) = in_order(refs[:-4]), refs[-4:]
    half, _ = place()
    groups, rows, full = waves_ref.shape
    block = full // 2

    @pl.when(half == 0)
    def _():
        for k, ref in enumerate(arrived[1:]):
            out_ref[(groups + k) * rows : (groups + k + 1) * rows, :] = ref[rows:, :]
        store_taps(
            [own_ref[:, m * block : (m + 1) * block] for m in range(taps_ref.shape[0])],
            table_ref,
            taps_ref,
        )
        store_waves([ref[:rows, :] for ref in arrived], table_ref, [waves_ref])
        products(waves_ref, taps_ref, groups, sums_ref)
        sums = sums_ref[...].reshape(groups * rows, full)
        out_ref[: groups * rows, :] = back_from(sums, table_ref).astype(jnp.bfloat16)


def store_parts(own, other, outs):
    half, group = place()
    rows = outs[0].shape[0] // HALVES
    for k, out_ref in enumerate(outs):
        out_ref[span(half, rows), :] = own(group ^ k).astype(jnp.bfloat16)
        out_ref[span(1 - half, rows), :] = other(group ^ k).astype(jnp.bfloat16)


def near_kernel(table_ref, own_ref, other_ref, gated_ref, skip_ref, *refs):
    groups = (len(refs) - 8) // 2
    arrived, parts = in_order(refs[:groups]), refs[groups : 2 * groups]
    taps_ref, sums_ref, out_ref, skipped_ref = refs[2 * groups : 2 * groups + 4]
    other_taps_ref, own_waves_ref, waves_ref, other_sums_ref = refs[2 * groups + 4 :]
    half, _ = place()
    _, rows, full = sums_ref.shape
    block = full // 2
    store_taps(
        [own_ref[:, m * block : (m + 1) * block] for m in range(taps_ref.shape[0])],
        table_ref,
        taps_ref,
    )
    other_taps = []
    for m in range(groups):
        other_taps.append(other_ref[(m + 1) * rows : (m + 2) * rows, :].astype(jnp.float32))
    store_taps(other_taps, table_ref, other_taps_ref)
    blocks = []
    for ref in arrived:
        blocks += [ref[span(half, rows), :], ref[span(1 - half, rows), :]]
    store_waves(blocks, table_ref, [own_waves_ref, waves_ref])
    products(own_waves_ref, taps_ref, 0, sums_ref)
    products(waves_ref, other_taps_ref, 0, other_sums_ref)
    spectra = [ref[...].reshape(groups * rows, full) for ref in (other_sums_ref, sums_ref)]
    out_ref[...] = back_from(jnp.concatenate(spectra, axis=0), table_ref).reshape(out_ref.shape)
    store_parts(lambda j: out_ref[groups + j], lambda j: out_ref[j], parts)
    spread = jnp.broadcast_to(skip_ref[...][None, :], (block, gated_ref.shape[0])).T
    skipped_ref[...] = spread * gated_ref[...].astype(jnp.float32)


def far_kernel(table_ref, taps_ref, sums_ref, other_ref, came_ref, across_ref, *refs):
    outs, (waves_ref, total_ref, own_ref) = refs[:-3], refs[-3:]
    groups, rows, full = sums_ref.shape
    blocks = [came_ref[:rows, :]]
    blocks += [across_ref[at * rows : (at + 1) * rows, :] for at in range(groups, 2 * groups - 1)]
    store_waves(blocks, table_ref, [waves_ref])
    products(waves_ref, taps_ref, groups, total_ref, sums_ref)
    total = total_ref[...].reshape(groups * rows, full)
    own_ref[...] = back_from(total, table_ref).reshape(own_ref.shape)

    def other(j):
        return other_ref[j] + across_ref[span(j, rows), :].astype(jnp.float32)

    store_parts(lambda j: own_ref[j], other, outs)


def join_kernel(*refs):
    parts, out_ref = in_order(refs[:-1]), refs[-1]
    groups = len(parts)
    _, group = place()
    rows = parts[0].shape[0] // HALVES
    for k, part_ref in enumerate(parts):
        for half in range(HALVES):
            out_ref[span(half * groups + (group ^ k), rows), :] = part_ref[
                half * rows : (half + 1) * rows, :
            ]


def copy_kernel(in_ref, out_ref):
    out_ref[...] = in_ref[...]


def final_kernel(queries_ref, skipped_ref, convolved_ref, out_ref):
    total = convolved_ref[...].astype(jnp.float32) + skipped_ref[...]
    out_ref[...] = (queries_ref[...].astype(jnp.float32) * total).astype(jnp.bfloat16)


VMEM = pl.BlockSpec(memory_space=pltpu.VMEM)
HBM = pl.BlockSpec(memory_space=pltpu.HBM)


def call(kernel, outs, args, scratch=(), far=0, cost=None):
    args = [
        pltpu.with_memory_space_constraint(arg, pltpu.HBM) if i < far else arg
        for i, arg in enumerate(args)
    ]
    return pl.pallas_call(
        kernel,
        out_shape=[jax.ShapeDtypeStruct(shape, dtype) for shape, dtype in outs],
        in_specs=[HBM if i < far else VMEM for i in range(len(args))],
        out_specs=[VMEM] * len(outs),
        scratch_shapes=list(scratch),
        cost_estimate=cost,
        compiler_params=pltpu.CompilerParams(vmem_limit_bytes=16 * 1024 * 1024),
    )(*args)


def per_device(queries, keys, values, filters, skip):
    channels, block = keys.shape
    shards = lax.axis_size(AXIS)
    groups = shards // HALVES
    rows = channels // shards
    chans = HALVES * rows
    full = 2 * block
    f32, bf16 = jnp.float32, jnp.bfloat16
    table = jnp.asarray(transform_table(block))
    swap = lambda x, k: lax.ppermute(x, AXIS, [(i, i ^ k) for i in range(shards)])
    whole = ((channels, block), bf16)
    group_part = ((chans, block), bf16)
    waves_of = ((groups, rows, full), f32)
    taps_of = lambda count: ((count, rows, full), f32)
    early_part = (((groups + 1) * rows, block), bf16)
    across_part = (((2 * groups - 1) * rows, block), bf16)
    outputs = ((shards, rows, block), f32)
    scratch = lambda *shapes: [pltpu.VMEM(*shape) for shape in shapes]

    queries, skip, gated, *sends = call(
        gate_kernel,
        [whole, (skip.shape, f32), whole] + [group_part] * groups,
        (keys, values, queries, skip),
        scratch(whole, whole) + [pltpu.SemaphoreType.DMA((4,))],
        4,
    )
    own = filters
    (coarse,) = call(coarse_kernel, [early_part], (own, sends[0]))
    other = swap(coarse, groups)
    arrived = [swap(sends[k], k) if k else sends[k] for k in partners(groups)]
    (lead,) = call(
        lead_kernel,
        [across_part],
        (table, own, *arrived),
        scratch(taps_of(shards), waves_of, waves_of),
    )
    across = swap(lead, groups)
    *parts, taps, sums, other_out, skipped = call(
        near_kernel,
        [group_part] * groups
        + [taps_of(shards), waves_of, outputs, ((channels, block), f32)],
        (table, own, other, gated, skip, *arrived),
        scratch(taps_of(groups), waves_of, waves_of, waves_of),
        cost=pl.CostEstimate(flops=2 * 10**8, transcendentals=0, bytes_accessed=0),
    )

    def give_back(parts):
        returned = [swap(parts[k], k) if k else parts[k] for k in partners(groups)]
        return call(join_kernel, [whole], returned)[0]

    def late(across):
        return give_back(
            call(
                far_kernel,
                [group_part] * groups,
                (table, taps, sums, other_out, other, across),
                scratch(waves_of, waves_of, ((groups, rows, block), f32)),
            )
        )

    copy = lambda x: call(copy_kernel, [whole], (x,))[0]
    first = lax.axis_index(AXIS) < groups
    convolved = lax.cond(first, lambda: give_back(parts), lambda: copy(gated))
    convolved = lax.cond(
        first, lambda done, _: copy(done), lambda _, across: late(across), convolved, across
    )
    return call(final_kernel, [whole], (queries, skipped, convolved))[0]


def solution(mesh):
    placed = (
        P("tensor", AXIS),
        P("tensor", AXIS),
        P("tensor", AXIS),
        P(("tensor", AXIS), None),
        P("tensor"),
    )
    return jax.shard_map(
        per_device, mesh=mesh, in_specs=placed, out_specs=P("tensor", AXIS), check_vma=False
    )
```

```python
import jax
import jax.numpy as jnp
import ml_dtypes
import numpy as np
from jax import lax
from jax.experimental import pallas as pl
from jax.experimental.pallas import tpu as pltpu
from jax.sharding import PartitionSpec as P

AXIS = "context"
HALVES = 2


def transform_table(block):
    angles = np.pi * np.outer(np.arange(block), 2 * np.arange(block) + 1) / (2 * block)
    table = np.concatenate([np.cos(angles), -np.sin(angles)], axis=1)
    high = table.astype(ml_dtypes.bfloat16)
    low = (table - high.astype(np.float64)).astype(ml_dtypes.bfloat16)
    return np.concatenate([high, low], axis=0)


def dot(left, right, turned=False):
    dims = (((1,), (1 if turned else 0,)), ((), ()))
    return lax.dot_general(left, right, dims, preferred_element_type=jnp.float32)


def split(values):
    high = values.astype(jnp.bfloat16)
    return high, (values - high.astype(jnp.float32)).astype(jnp.bfloat16)


def partners(groups):
    return (groups - 1, *range(1, groups - 1), 0)


def in_order(refs):
    order = partners(len(refs))
    return [refs[order.index(k)] for k in range(len(refs))]


def place():
    index = lax.axis_index(AXIS)
    groups = lax.axis_size(AXIS) // HALVES
    return index // groups, lax.rem(index, groups)


def span(start, size):
    return pl.ds(pl.multiple_of(start * size, size), size)


def store_waves(blocks, table_ref, waves_refs):
    _, group = place()
    rows = waves_refs[0].shape[1]
    stacked = jnp.concatenate(blocks, axis=0)
    spectra = dot(jnp.concatenate([stacked, stacked], axis=1), table_ref[...])
    parts = len(waves_refs)
    for k in range(len(blocks) // parts):
        for i, ref in enumerate(waves_refs):
            at = (k * parts + i) * rows
            ref[group ^ k] = spectra[at : at + rows]


def store_taps(taps, table_ref, taps_ref):
    count, rows, full = taps_ref.shape
    block = full // 2
    high, low = split(jnp.concatenate(taps, axis=0))
    spectra = dot(jnp.concatenate([high, high], axis=1), table_ref[...]) + dot(
        low, table_ref[:block, :]
    )
    odd = lax.rem(lax.broadcasted_iota(jnp.int32, (rows, block), 1), 2)
    sign = 1.0 - 2.0 * odd.astype(jnp.float32)
    for m in range(count):
        now = spectra[m * rows : (m + 1) * rows]
        if m == 0:
            taps_ref[m] = now
            continue
        past = spectra[(m - 1) * rows : m * rows]
        taps_ref[m, :, :block] = now[:, :block] - sign * past[:, block:]
        taps_ref[m, :, block:] = now[:, block:] + sign * past[:, :block]


def back_from(spectra, table_ref):
    block = spectra.shape[1] // 2
    high, low = split(spectra)
    top, rest = table_ref[:block, :], table_ref[block:, :]
    total = dot(high, top, True) + dot(low, top, True) + dot(high, rest, True)
    return total * (1.0 / block)


def stacked_back_from(spectra, table_ref):
    count, block = spectra.shape[0], spectra.shape[1] // 2
    both = dot(jnp.concatenate(split(spectra), axis=0), table_ref[...], True)
    total = both[:count, :block] + both[count:, :block] + both[:count, block:]
    return total * (1.0 / block)


def products(waves_ref, taps_ref, shift, out_ref, start=None):
    groups, rows, full = waves_ref.shape
    block = full // 2
    for at in range(0, rows, 8):
        part = slice(at, at + 8)
        waves = [waves_ref[b, part, :] for b in range(groups)]
        for j in range(groups):
            total = [None, None]
            if start is not None:
                total = [start[j, part, :block], start[j, part, block:]]
            for b in range(groups):
                if shift + j < b:
                    continue
                tap = taps_ref[shift + j - b, part, :]
                re, im = waves[b][:, :block], waves[b][:, block:]
                tap_re, tap_im = tap[:, :block], tap[:, block:]
                new = [re * tap_re - im * tap_im, re * tap_im + im * tap_re]
                total = [n if t is None else t + n for t, n in zip(total, new)]
            out_ref[j, part, :block] = total[0]
            out_ref[j, part, block:] = total[1]


def gate_kernel(*refs):
    sources, targets, gated_ref = refs[:4], refs[4:6], refs[6]
    sends, (keys_ref, values_ref, sem) = refs[7:-3], refs[-3:]
    copies = [
        pltpu.make_async_copy(source, target, sem.at[i])
        for i, (source, target) in enumerate(zip(sources, (keys_ref, values_ref, *targets)))
    ]
    for copy in copies:
        copy.start()
    copies[0].wait()
    copies[1].wait()
    gated_ref[...] = (
        keys_ref[...].astype(jnp.float32) * values_ref[...].astype(jnp.float32)
    ).astype(jnp.bfloat16)
    groups = len(sends)
    _, group = place()
    rows = sends[0].shape[0] // HALVES
    for k, send_ref in enumerate(sends):
        for part in range(HALVES):
            send_ref[part * rows : (part + 1) * rows, :] = gated_ref[
                span(part * groups + (group ^ k), rows), :
            ]
    for copy in copies[2:]:
        copy.wait()


def coarse_kernel(near_ref, stays_ref, coarse_ref):
    half, _ = place()
    chans, block = stays_ref.shape
    rows = chans // HALVES
    groups = near_ref.shape[1] // block // HALVES
    coarse_ref[:rows, :] = stays_ref[span(1 - half, rows), :]
    for m in range(groups):
        parts = split(near_ref[:, m * block : (m + 1) * block])
        coarse_ref[(m + 1) * rows : (m + 2) * rows, :] = parts[0]
        at = (groups + 1 + m) * rows
        if at < coarse_ref.shape[0]:
            coarse_ref[at : at + rows, :] = parts[1]


def lead_kernel(table_ref, own_ref, *refs):
    arrived, (out_ref, taps_ref, waves_ref, sums_ref) = in_order(refs[:-4]), refs[-4:]
    half, _ = place()
    groups, rows, full = waves_ref.shape
    block = full // 2

    @pl.when(half == 0)
    def _():
        for k, ref in enumerate(arrived[1:]):
            out_ref[(groups + k) * rows : (groups + k + 1) * rows, :] = ref[rows:, :]
        store_taps(
            [own_ref[:, m * block : (m + 1) * block] for m in range(taps_ref.shape[0])],
            table_ref,
            taps_ref,
        )
        store_waves([ref[:rows, :] for ref in arrived], table_ref, [waves_ref])
        products(waves_ref, taps_ref, groups, sums_ref)
        sums = sums_ref[...].reshape(groups * rows, full)
        out_ref[: groups * rows, :] = back_from(sums, table_ref).astype(jnp.bfloat16)


def store_parts(own, other, outs):
    half, group = place()
    rows = outs[0].shape[0] // HALVES
    for k, out_ref in enumerate(outs):
        out_ref[span(half, rows), :] = own(group ^ k).astype(jnp.bfloat16)
        out_ref[span(1 - half, rows), :] = other(group ^ k).astype(jnp.bfloat16)


def near_kernel(table_ref, own_ref, other_ref, gated_ref, skip_ref, *refs):
    groups = (len(refs) - 8) // 2
    arrived, parts = in_order(refs[:groups]), refs[groups : 2 * groups]
    taps_ref, sums_ref, out_ref, skipped_ref = refs[2 * groups : 2 * groups + 4]
    other_taps_ref, own_waves_ref, waves_ref, other_sums_ref = refs[2 * groups + 4 :]
    half, _ = place()
    _, rows, full = sums_ref.shape
    block = full // 2
    store_taps(
        [own_ref[:, m * block : (m + 1) * block] for m in range(taps_ref.shape[0])],
        table_ref,
        taps_ref,
    )
    other_taps = []
    for m in range(groups):
        tap = other_ref[(m + 1) * rows : (m + 2) * rows, :].astype(jnp.float32)
        at = (groups + 1 + m) * rows
        if at < other_ref.shape[0]:
            tap = tap + other_ref[at : at + rows, :].astype(jnp.float32)
        other_taps.append(tap)
    store_taps(other_taps, table_ref, other_taps_ref)
    blocks = []
    for ref in arrived:
        blocks += [ref[span(half, rows), :], ref[span(1 - half, rows), :]]
    store_waves(blocks, table_ref, [own_waves_ref, waves_ref])
    products(own_waves_ref, taps_ref, 0, sums_ref)
    products(waves_ref, other_taps_ref, 0, other_sums_ref)
    spectra = [ref[...].reshape(groups * rows, full) for ref in (other_sums_ref, sums_ref)]
    out_ref[...] = back_from(jnp.concatenate(spectra, axis=0), table_ref).reshape(out_ref.shape)
    store_parts(lambda j: out_ref[groups + j], lambda j: out_ref[j], parts)
    spread = jnp.broadcast_to(skip_ref[...][None, :], (block, gated_ref.shape[0])).T
    skipped_ref[...] = spread * gated_ref[...].astype(jnp.float32)


def far_kernel(table_ref, taps_ref, sums_ref, other_ref, came_ref, across_ref, *refs):
    outs, (waves_ref, total_ref, own_ref) = refs[:-3], refs[-3:]
    groups, rows, full = sums_ref.shape
    blocks = [came_ref[:rows, :]]
    blocks += [across_ref[at * rows : (at + 1) * rows, :] for at in range(groups, 2 * groups - 1)]
    store_waves(blocks, table_ref, [waves_ref])
    products(waves_ref, taps_ref, groups, total_ref, sums_ref)
    total = total_ref[...].reshape(groups * rows, full)
    own_ref[...] = stacked_back_from(total, table_ref).reshape(own_ref.shape)

    def other(j):
        return other_ref[j] + across_ref[span(j, rows), :].astype(jnp.float32)

    store_parts(lambda j: own_ref[j], other, outs)


def join_kernel(*refs):
    parts, out_ref = in_order(refs[:-1]), refs[-1]
    groups = len(parts)
    _, group = place()
    rows = parts[0].shape[0] // HALVES
    for k, part_ref in enumerate(parts):
        for half in range(HALVES):
            out_ref[span(half * groups + (group ^ k), rows), :] = part_ref[
                half * rows : (half + 1) * rows, :
            ]


def copy_kernel(in_ref, out_ref):
    out_ref[...] = in_ref[...]


def final_kernel(queries_ref, skipped_ref, convolved_ref, out_ref):
    total = convolved_ref[...].astype(jnp.float32) + skipped_ref[...]
    out_ref[...] = (queries_ref[...].astype(jnp.float32) * total).astype(jnp.bfloat16)


VMEM = pl.BlockSpec(memory_space=pltpu.VMEM)
HBM = pl.BlockSpec(memory_space=pltpu.HBM)


def call(kernel, outs, args, scratch=(), far=0):
    args = [
        pltpu.with_memory_space_constraint(arg, pltpu.HBM) if i < far else arg
        for i, arg in enumerate(args)
    ]
    return pl.pallas_call(
        kernel,
        out_shape=[jax.ShapeDtypeStruct(shape, dtype) for shape, dtype in outs],
        in_specs=[HBM if i < far else VMEM for i in range(len(args))],
        out_specs=[VMEM] * len(outs),
        scratch_shapes=list(scratch),
        compiler_params=pltpu.CompilerParams(vmem_limit_bytes=16 * 1024 * 1024),
    )(*args)


def per_device(queries, keys, values, filters, skip):
    channels, block = keys.shape
    shards = lax.axis_size(AXIS)
    groups = shards // HALVES
    rows = channels // shards
    chans = HALVES * rows
    full = 2 * block
    f32, bf16 = jnp.float32, jnp.bfloat16
    table = jnp.asarray(transform_table(block))
    swap = lambda x, k: lax.ppermute(x, AXIS, [(i, i ^ k) for i in range(shards)])
    whole = ((channels, block), bf16)
    group_part = ((chans, block), bf16)
    waves_of = ((groups, rows, full), f32)
    taps_of = lambda count: ((count, rows, full), f32)
    across_part = (((2 * groups - 1) * rows, block), bf16)
    outputs = ((shards, rows, block), f32)
    scratch = lambda *shapes: [pltpu.VMEM(*shape) for shape in shapes]

    queries, skip, gated, *sends = call(
        gate_kernel,
        [whole, (skip.shape, f32), whole] + [group_part] * groups,
        (keys, values, queries, skip),
        scratch(whole, whole) + [pltpu.SemaphoreType.DMA((4,))],
        4,
    )
    own = filters
    (coarse,) = call(coarse_kernel, [across_part], (own, sends[0]))
    other = swap(coarse, groups)
    arrived = [swap(sends[k], k) if k else sends[k] for k in partners(groups)]
    (lead,) = call(
        lead_kernel,
        [across_part],
        (table, own, *arrived),
        scratch(taps_of(shards), waves_of, waves_of),
    )
    across = swap(lead, groups)
    *parts, taps, sums, other_out, skipped = call(
        near_kernel,
        [group_part] * groups
        + [taps_of(shards), waves_of, outputs, ((channels, block), f32)],
        (table, own, other, gated, skip, *arrived),
        scratch(taps_of(groups), waves_of, waves_of, waves_of),
    )

    def give_back(parts):
        returned = [swap(parts[k], k) if k else parts[k] for k in partners(groups)]
        return call(join_kernel, [whole], returned)[0]

    def late(across):
        return give_back(
            call(
                far_kernel,
                [group_part] * groups,
                (table, taps, sums, other_out, other, across),
                scratch(waves_of, waves_of, ((groups, rows, block), f32)),
            )
        )

    copy = lambda x: call(copy_kernel, [whole], (x,))[0]
    first = lax.axis_index(AXIS) < groups
    convolved = lax.cond(first, lambda: give_back(parts), lambda: copy(gated))
    convolved = lax.cond(
        first, lambda done, _: copy(done), lambda _, across: late(across), convolved, across
    )
    return call(final_kernel, [whole], (queries, skipped, convolved))[0]


def solution(mesh):
    placed = (
        P("tensor", AXIS),
        P("tensor", AXIS),
        P("tensor", AXIS),
        P(("tensor", AXIS), None),
        P("tensor"),
    )
    return jax.shard_map(
        per_device, mesh=mesh, in_specs=placed, out_specs=P("tensor", AXIS), check_vma=False
    )
```

```python
import jax
import jax.numpy as jnp
import ml_dtypes
import numpy as np
from jax import lax
from jax.experimental import pallas as pl
from jax.experimental.pallas import tpu as pltpu
from jax.sharding import PartitionSpec as P

AXIS = "context"
HALVES = 2


def transform_table(block):
    angles = np.pi * np.outer(np.arange(block), 2 * np.arange(block) + 1) / (2 * block)
    table = np.concatenate([np.cos(angles), -np.sin(angles)], axis=1)
    high = table.astype(ml_dtypes.bfloat16)
    low = (table - high.astype(np.float64)).astype(ml_dtypes.bfloat16)
    return np.concatenate([high, low], axis=0)


def dot(left, right, turned=False):
    dims = (((1,), (1 if turned else 0,)), ((), ()))
    return lax.dot_general(left, right, dims, preferred_element_type=jnp.float32)


def split(values):
    high = values.astype(jnp.bfloat16)
    return high, (values - high.astype(jnp.float32)).astype(jnp.bfloat16)


def partners(groups):
    return (groups - 1, *range(1, groups - 1), 0)


def in_order(refs):
    order = partners(len(refs))
    return [refs[order.index(k)] for k in range(len(refs))]


def place():
    index = lax.axis_index(AXIS)
    groups = lax.axis_size(AXIS) // HALVES
    return index // groups, lax.rem(index, groups)


def span(start, size):
    return pl.ds(pl.multiple_of(start * size, size), size)


def store_waves(blocks, table_ref, waves_refs):
    _, group = place()
    rows = waves_refs[0].shape[1]
    stacked = jnp.concatenate(blocks, axis=0)
    spectra = dot(jnp.concatenate([stacked, stacked], axis=1), table_ref[...])
    parts = len(waves_refs)
    for k in range(len(blocks) // parts):
        for i, ref in enumerate(waves_refs):
            at = (k * parts + i) * rows
            ref[group ^ k] = spectra[at : at + rows]


def store_taps(taps, table_ref, taps_ref):
    count, rows, full = taps_ref.shape
    block = full // 2
    high, low = split(jnp.concatenate(taps, axis=0))
    spectra = dot(jnp.concatenate([high, high], axis=1), table_ref[...]) + dot(
        low, table_ref[:block, :]
    )
    odd = lax.rem(lax.broadcasted_iota(jnp.int32, (rows, block), 1), 2)
    sign = 1.0 - 2.0 * odd.astype(jnp.float32)
    for m in range(count):
        now = spectra[m * rows : (m + 1) * rows]
        if m == 0:
            taps_ref[m] = now
            continue
        past = spectra[(m - 1) * rows : m * rows]
        taps_ref[m, :, :block] = now[:, :block] - sign * past[:, block:]
        taps_ref[m, :, block:] = now[:, block:] + sign * past[:, :block]


def back_from(spectra, table_ref):
    block = spectra.shape[1] // 2
    high, low = split(spectra)
    top, rest = table_ref[:block, :], table_ref[block:, :]
    total = dot(high, top, True) + dot(low, top, True) + dot(high, rest, True)
    return total * (1.0 / block)


def stacked_back_from(spectra, table_ref):
    count, block = spectra.shape[0], spectra.shape[1] // 2
    both = dot(jnp.concatenate(split(spectra), axis=0), table_ref[...], True)
    total = both[:count, :block] + both[count:, :block] + both[:count, block:]
    return total * (1.0 / block)


def products(waves_ref, taps_ref, shift, out_ref, start=None):
    groups, rows, full = waves_ref.shape
    block = full // 2
    for at in range(0, rows, 8):
        part = slice(at, at + 8)
        waves = [waves_ref[b, part, :] for b in range(groups)]
        for j in range(groups):
            total = [None, None]
            if start is not None:
                total = [start[j, part, :block], start[j, part, block:]]
            for b in range(groups):
                if shift + j < b:
                    continue
                tap = taps_ref[shift + j - b, part, :]
                re, im = waves[b][:, :block], waves[b][:, block:]
                tap_re, tap_im = tap[:, :block], tap[:, block:]
                new = [re * tap_re - im * tap_im, re * tap_im + im * tap_re]
                total = [n if t is None else t + n for t, n in zip(total, new)]
            out_ref[j, part, :block] = total[0]
            out_ref[j, part, block:] = total[1]


def gate_kernel(*refs):
    sources, targets, gated_ref = refs[:4], refs[4:6], refs[6]
    sends, (keys_ref, values_ref, sem) = refs[7:-3], refs[-3:]
    copies = [
        pltpu.make_async_copy(source, target, sem.at[i])
        for i, (source, target) in enumerate(zip(sources, (keys_ref, values_ref, *targets)))
    ]
    for copy in copies:
        copy.start()
    copies[0].wait()
    copies[1].wait()
    gated_ref[...] = (
        keys_ref[...].astype(jnp.float32) * values_ref[...].astype(jnp.float32)
    ).astype(jnp.bfloat16)
    groups = len(sends)
    _, group = place()
    rows = sends[0].shape[0] // HALVES
    for k, send_ref in enumerate(sends):
        for part in range(HALVES):
            send_ref[part * rows : (part + 1) * rows, :] = gated_ref[
                span(part * groups + (group ^ k), rows), :
            ]
    for copy in copies[2:]:
        copy.wait()


def coarse_kernel(near_ref, stays_ref, coarse_ref):
    half, _ = place()
    chans, block = stays_ref.shape
    rows = chans // HALVES
    groups = near_ref.shape[1] // block // HALVES
    coarse_ref[:rows, :] = stays_ref[span(1 - half, rows), :]
    for m in range(groups):
        parts = split(near_ref[:, m * block : (m + 1) * block])
        coarse_ref[(m + 1) * rows : (m + 2) * rows, :] = parts[0]
        at = (groups + 1 + m) * rows
        if at < coarse_ref.shape[0]:
            coarse_ref[at : at + rows, :] = parts[1]


def lead_kernel(table_ref, own_ref, *refs):
    arrived, (out_ref, taps_ref, waves_ref, sums_ref) = in_order(refs[:-4]), refs[-4:]
    half, _ = place()
    groups, rows, full = waves_ref.shape
    block = full // 2

    @pl.when(half == 0)
    def _():
        for k, ref in enumerate(arrived[1:]):
            out_ref[(groups + k) * rows : (groups + k + 1) * rows, :] = ref[rows:, :]
        store_taps(
            [own_ref[:, m * block : (m + 1) * block] for m in range(taps_ref.shape[0])],
            table_ref,
            taps_ref,
        )
        store_waves([ref[:rows, :] for ref in arrived], table_ref, [waves_ref])
        products(waves_ref, taps_ref, groups, sums_ref)
        sums = sums_ref[...].reshape(groups * rows, full)
        out_ref[: groups * rows, :] = back_from(sums, table_ref).astype(jnp.bfloat16)


def store_parts(own, other, outs):
    half, group = place()
    rows = outs[0].shape[0] // HALVES
    for k, out_ref in enumerate(outs):
        out_ref[span(half, rows), :] = own(group ^ k).astype(jnp.bfloat16)
        out_ref[span(1 - half, rows), :] = other(group ^ k).astype(jnp.bfloat16)


def near_kernel(table_ref, own_ref, other_ref, gated_ref, skip_ref, *refs):
    groups = (len(refs) - 8) // 2
    arrived, parts = in_order(refs[:groups]), refs[groups : 2 * groups]
    taps_ref, sums_ref, out_ref, skipped_ref = refs[2 * groups : 2 * groups + 4]
    other_taps_ref, own_waves_ref, waves_ref, other_sums_ref = refs[2 * groups + 4 :]
    half, _ = place()
    _, rows, full = sums_ref.shape
    block = full // 2
    store_taps(
        [own_ref[:, m * block : (m + 1) * block] for m in range(taps_ref.shape[0])],
        table_ref,
        taps_ref,
    )
    other_taps = []
    for m in range(groups):
        tap = other_ref[(m + 1) * rows : (m + 2) * rows, :].astype(jnp.float32)
        at = (groups + 1 + m) * rows
        if at < other_ref.shape[0]:
            tap = tap + other_ref[at : at + rows, :].astype(jnp.float32)
        other_taps.append(tap)
    store_taps(other_taps, table_ref, other_taps_ref)
    blocks = []
    for ref in arrived:
        blocks += [ref[span(half, rows), :], ref[span(1 - half, rows), :]]
    store_waves(blocks, table_ref, [own_waves_ref, waves_ref])
    products(own_waves_ref, taps_ref, 0, sums_ref)
    products(waves_ref, other_taps_ref, 0, other_sums_ref)
    spectra = [ref[...].reshape(groups * rows, full) for ref in (other_sums_ref, sums_ref)]
    out_ref[...] = back_from(jnp.concatenate(spectra, axis=0), table_ref).reshape(out_ref.shape)
    store_parts(lambda j: out_ref[groups + j], lambda j: out_ref[j], parts)
    spread = jnp.broadcast_to(skip_ref[...][None, :], (block, gated_ref.shape[0])).T
    skipped_ref[...] = spread * gated_ref[...].astype(jnp.float32)


def far_kernel(table_ref, taps_ref, sums_ref, other_ref, came_ref, across_ref, *refs):
    outs, (waves_ref, total_ref, own_ref) = refs[:-3], refs[-3:]
    groups, rows, full = sums_ref.shape
    blocks = [came_ref[:rows, :]]
    blocks += [across_ref[at * rows : (at + 1) * rows, :] for at in range(groups, 2 * groups - 1)]
    store_waves(blocks, table_ref, [waves_ref])
    products(waves_ref, taps_ref, groups, total_ref, sums_ref)
    total = total_ref[...].reshape(groups * rows, full)
    own_ref[...] = stacked_back_from(total, table_ref).reshape(own_ref.shape)

    def other(j):
        return other_ref[j] + across_ref[span(j, rows), :].astype(jnp.float32)

    store_parts(lambda j: own_ref[j], other, outs)


def join_kernel(*refs):
    parts, out_ref = in_order(refs[:-1]), refs[-1]
    groups = len(parts)
    _, group = place()
    rows = parts[0].shape[0] // HALVES
    for k, part_ref in enumerate(parts):
        for half in range(HALVES):
            out_ref[span(half * groups + (group ^ k), rows), :] = part_ref[
                half * rows : (half + 1) * rows, :
            ]


def copy_kernel(in_ref, out_ref):
    out_ref[...] = in_ref[...]


def final_kernel(queries_ref, skipped_ref, convolved_ref, out_ref):
    total = convolved_ref[...].astype(jnp.float32) + skipped_ref[...]
    out_ref[...] = (queries_ref[...].astype(jnp.float32) * total).astype(jnp.bfloat16)


VMEM = pl.BlockSpec(memory_space=pltpu.VMEM)
HBM = pl.BlockSpec(memory_space=pltpu.HBM)


def call(kernel, outs, args, scratch=(), far=0):
    args = [
        pltpu.with_memory_space_constraint(arg, pltpu.HBM) if i < far else arg
        for i, arg in enumerate(args)
    ]
    return pl.pallas_call(
        kernel,
        out_shape=[jax.ShapeDtypeStruct(shape, dtype) for shape, dtype in outs],
        in_specs=[HBM if i < far else VMEM for i in range(len(args))],
        out_specs=[VMEM] * len(outs),
        scratch_shapes=list(scratch),
        compiler_params=pltpu.CompilerParams(vmem_limit_bytes=16 * 1024 * 1024),
    )(*args)


def per_device(queries, keys, values, filters, skip):
    channels, block = keys.shape
    shards = lax.axis_size(AXIS)
    groups = shards // HALVES
    rows = channels // shards
    chans = HALVES * rows
    full = 2 * block
    f32, bf16 = jnp.float32, jnp.bfloat16
    table = jnp.asarray(transform_table(block))
    swap = lambda x, k: lax.ppermute(x, AXIS, [(i, i ^ k) for i in range(shards)])
    whole = ((channels, block), bf16)
    group_part = ((chans, block), bf16)
    waves_of = ((groups, rows, full), f32)
    taps_of = lambda count: ((count, rows, full), f32)
    across_part = (((2 * groups - 1) * rows, block), bf16)
    outputs = ((shards, rows, block), f32)
    scratch = lambda *shapes: [pltpu.VMEM(*shape) for shape in shapes]

    queries, skip, gated, *sends = call(
        gate_kernel,
        [whole, (skip.shape, f32), whole] + [group_part] * groups,
        (keys, values, queries, skip),
        scratch(whole, whole) + [pltpu.SemaphoreType.DMA((4,))],
        4,
    )
    own = filters
    (coarse,) = call(coarse_kernel, [across_part], (own, sends[0]))
    other = swap(coarse, groups)
    arrived = [swap(sends[k], k) if k else sends[k] for k in partners(groups)]
    (lead,) = call(
        lead_kernel,
        [across_part],
        (table, own, *arrived),
        scratch(taps_of(shards), waves_of, waves_of),
    )
    across = swap(lead, groups)
    *parts, taps, sums, other_out, skipped = call(
        near_kernel,
        [group_part] * groups
        + [taps_of(shards), waves_of, outputs, ((channels, block), f32)],
        (table, own, other, gated, skip, *arrived),
        scratch(taps_of(groups), waves_of, waves_of, waves_of),
    )

    def give_back(parts, order):
        returned = [swap(parts[k], k) if k else parts[k] for k in order]

        def join(*refs):
            join_kernel(*[refs[order.index(k)] for k in partners(groups)], refs[-1])

        return call(join, [whole], returned)[0]

    def late(across):
        return give_back(
            call(
                far_kernel,
                [group_part] * groups,
                (table, taps, sums, other_out, other, across),
                scratch(waves_of, waves_of, ((groups, rows, block), f32)),
            ),
            partners(groups),
        )

    copy = lambda x: call(copy_kernel, [whole], (x,))[0]
    near_first = (1, groups - 1, *range(2, groups - 1), 0)
    first = lax.axis_index(AXIS) < groups
    convolved = lax.cond(first, lambda: give_back(parts, near_first), lambda: copy(gated))
    convolved = lax.cond(
        first, lambda done, _: copy(done), lambda _, across: late(across), convolved, across
    )
    return call(final_kernel, [whole], (queries, skipped, convolved))[0]


def solution(mesh):
    placed = (
        P("tensor", AXIS),
        P("tensor", AXIS),
        P("tensor", AXIS),
        P(("tensor", AXIS), None),
        P("tensor"),
    )
    return jax.shard_map(
        per_device, mesh=mesh, in_specs=placed, out_specs=P("tensor", AXIS), check_vma=False
    )
```
